128 devices in a mesh: rep: 4 (over z), ten: 32 (over x, y, core).
Axes of the slice: x: 4, y: 4, z: 4, core: 2. Of those that a mesh axis runs over, the one named last changes fastest.
Arguments:
- blocks: bfloat16 [64, 512, 4096], P(None, 'ten'), may hold values from -0.5 to 0.5
- col_counts: int32 [32], replicated, may hold values from 1 to 4, 64 in all
- block_sizes: int32 [32], replicated, may hold values from 32 to 64
- occ_coeff: bfloat16 [2048, 256], P(None, 'rep'), may hold values from -1.5 to 1.5
- occ_weight: float32 [256], P('rep'), may hold values from 0.1 to 1
- virt_green: bfloat16 [2048, 2048], replicated, may hold values from -0.125 to 0.125
Outputs:
- chi: float32 [512, 512], P('ten')
The draws below stay inside these ranges and needn't reach their ends.
Inputs may be any that keep to these rules, and one draw needn't show every extreme that they name: `col_counts`: each block column holds 1 to 4 nonzero blocks, 64 in all, and some column holds exactly 4.
All inputs are finite; a program needn't handle non-finite values.
Results may differ from the reference program's by a relative error of at most 0.0047.
Values may be sent and summed in bfloat16 or wider, within the bound.
No kernel may reach another device: no remote copies, remote signals or barrier semaphores. Data moves between devices by JAX's collectives and lax.ppermute only.
A program may use at most 192 MiB of HBM per device.

```python
import math
import jax
import jax.numpy as jnp
import numpy as np
from jax import lax

BS = 64
OCC_REP = 64
PC = 2
MOST = 4
NB = 32
NAO = 2048
NPAIR = 64
NAUX = 512
NOCC = 256
N_REP = 4


def touch_ends(entries, key, low, largest):
    place = [jax.random.randint(jax.random.fold_in(key, axis), (), 0, length) for axis, length in enumerate(entries.shape)]
    widest = entries.shape.index(max(entries.shape))
    neighbour = place[:widest] + [(place[widest] + 1) % entries.shape[widest]] + place[widest + 1:]
    return entries.at[tuple(place)].set(low).at[tuple(neighbour)].set(largest)


def level_of(stream_key, shape, cuts, low, high):
    factor_of, own = 1.0, jax.random.fold_in(stream_key, 6)
    for dim, shards_of in cuts:
        steps = jnp.exp(jax.random.uniform(jax.random.fold_in(own, dim), (shards_of,), jnp.float32, low / len(cuts), high / len(cuts)))
        factor_of = factor_of * jnp.repeat(steps, shape[dim] // shards_of).reshape([-1 if axis == dim else 1 for axis in range(len(shape))])
    return factor_of


def length_profile(count, total, bound, slope):
    portions = [(1 << 20) // math.isqrt(grade ** slope) + 1 for grade in range(2, count + 1)]
    spare, holding = total - bound - (count - 1), [1] * (count - 1)
    while spare > 0:
        movable = [i for i in range(count - 1) if holding[i] < bound]
        pool, remaining = sum([portions[i] for i in movable]), spare
        for i in movable:
            more = min(bound - holding[i], max(1, remaining * portions[i] // pool), spare)
            holding[i] = holding[i] + more
            spare = spare - more
    return np.array([bound] + holding)


def ragged(rng, count, total, reach, skew):
    if count == 2:
        one = jax.random.randint(rng, (), max(1, total - reach), min(reach, total - 1) + 1)
        return jnp.stack([one, total - one])
    lengths = jnp.asarray(length_profile(count, total, reach, skew), jnp.int32)
    pairs = (count - 1) // 2
    donor, receiver = lengths[1:1 + 2 * pairs:2], lengths[2:2 + 2 * pairs:2]
    margin = jnp.minimum(donor - 1, reach - receiver)
    moved = jax.random.randint(jax.random.fold_in(rng, 1), (pairs,), 0, 1 << 20) % (margin + 1)
    lengths = lengths.at[1:1 + 2 * pairs:2].set(donor - moved).at[2:2 + 2 * pairs:2].set(receiver + moved)
    return lengths[jax.random.permutation(jax.random.fold_in(rng, 2), count)]


def normal_values(own_key, dims, width, limit, cuts=(), held_as=jnp.bfloat16):
    factor_of = level_of(own_key, dims, cuts, -0.22, 0.18) if cuts else 1.0
    drawn = jax.random.normal(own_key, dims, jnp.float32) * width * factor_of
    return jnp.minimum(jnp.maximum(drawn, -limit), limit).astype(held_as)


def setup_inputs(seed: int = 0) -> dict:
    streams_of = jax.random.split(jax.random.key(seed), 7)
    return {
        "blocks": normal_values(streams_of[0], (NPAIR, NAUX, BS * BS), (1.0 / (NPAIR * BS * BS * N_REP) ** 0.25), 0.5, ((1, 32),)),
        "col_counts": ragged(streams_of[1], NB, NPAIR, MOST, 2).astype(jnp.int32),
        "block_sizes": touch_ends(jax.random.randint(streams_of[2], (NB,), BS // 2, BS + 1), jax.random.fold_in(streams_of[2], 1), BS // 2, BS).astype(jnp.int32),
        "occ_coeff": normal_values(streams_of[3], (NAO, NOCC), (1.0 / (OCC_REP * PC * BS) ** 0.25), 1.5, ((1, 4),)),
        "occ_weight": jnp.clip(jnp.exp(math.log(1.0) - 2.3025851 * jax.random.uniform(streams_of[4], (NOCC,), jnp.float32) ** level_of(streams_of[4], (NOCC,), ((0, 4),), -0.2, 0.2)), 0.1, 1.0),
        "virt_green": normal_values(streams_of[5], (NAO, NAO), NAO ** -0.5, 0.125),
    }


def pattern(col_counts, pair_count, block_count):
    pair_index = jnp.arange(pair_count, dtype=jnp.int32)
    ends = jnp.cumsum(col_counts).astype(jnp.int32)
    col_block = jnp.sum((ends[None, :] <= pair_index[:, None]).astype(jnp.int32), axis=1).astype(jnp.int32)
    starts = (ends - col_counts).astype(jnp.int32)
    col_rank = (pair_index - jnp.take(starts, col_block)).astype(jnp.int32)
    offset = ((col_rank + 1) // 2) * jnp.where(col_rank % 2 == 1, 1, -1)
    row_block = ((col_block + offset) % block_count).astype(jnp.int32)
    return row_block, col_block, col_rank


def reference(blocks, col_counts, block_sizes, occ_coeff, occ_weight, virt_green):
    row_block, col_block, col_rank = pattern(col_counts, NPAIR, NB)
    in_block = (jnp.arange(BS)[None, :] < block_sizes[:, None]).astype(jnp.bfloat16)
    masked = blocks.reshape(NPAIR, NAUX, BS, BS) * (in_block[row_block][:, None, :, None] * in_block[col_block][:, None, None, :])
    col_hot = (col_block[:, None] == jnp.arange(NB)[None, :]).astype(jnp.float32)
    chi = jnp.zeros((NAUX, NAUX), jnp.float32)
    for replica in range(N_REP):
        coeff = occ_coeff[:, replica * OCC_REP:(replica + 1) * OCC_REP]
        weight = occ_weight[replica * OCC_REP:(replica + 1) * OCC_REP]
        occ_rows = coeff.reshape(NB, BS, OCC_REP)[row_block].astype(jnp.float32)
        partial_value = jnp.einsum('kxi,kpxy->kpiy', occ_rows, masked.astype(jnp.float32))
        summed = jnp.einsum('kb,kpiy->piby', col_hot, partial_value, precision=lax.Precision.HIGHEST)
        half = summed.astype(jnp.bfloat16).reshape(NAUX, OCC_REP * NAO)
        folded = (summed * weight[None, :, None, None]).astype(jnp.bfloat16).reshape(NAUX * OCC_REP, NAO)
        dressed = jnp.dot(folded, virt_green, preferred_element_type=jnp.float32).astype(jnp.bfloat16)
        dressed = dressed.reshape(NAUX, OCC_REP * NAO)
        chi = chi + jnp.dot(half, dressed.T, preferred_element_type=jnp.float32)
    return chi
```

```python
import functools

import jax
import jax.numpy as jnp
from jax import lax
from jax.experimental import pallas as pl
from jax.experimental.pallas import tpu as pltpu
from jax.sharding import PartitionSpec as P

BS = 64
MOST = 4
LANES = 128
MIB = 1024 * 1024


def half_kernel(counts_ref, sizes_ref, occ_ref, blocks_ref, out_ref, slots, turned, starts):
    block_count = counts_ref.shape[0]
    aux_rows = blocks_ref.shape[1]
    occ_count = BS
    half_x = BS // 2

    def count_up(b, total):
        starts[b] = total
        return total + counts_ref[b]

    lax.fori_loop(0, block_count, count_up, jnp.int32(0))
    slots[...] = jnp.zeros_like(slots)

    x_of = 2 * lax.broadcasted_iota(jnp.int32, (half_x, LANES), 0) + (
        lax.broadcasted_iota(jnp.int32, (half_x, LANES), 1) // BS
    )
    lane = lax.broadcasted_iota(jnp.int32, (BS, LANES), 1)
    low = lane < BS

    def column_pair(m, carry):
        weights = []
        for side in range(2):
            b = 2 * m + side
            first, count = starts[b], counts_ref[b]
            rows = []
            for j in range(MOST):
                offset = (j + 1) // 2 if j % 2 == 1 else -(j // 2)
                row = lax.rem(b + offset + block_count, block_count)
                size = jnp.where(j < count, sizes_ref[row], 0)
                coeff = occ_ref[pl.ds(row * half_x, half_x), :]
                rows.append(jnp.where(x_of < size, coeff, 0.0))

                @pl.when(j < count)
                def _(side=side, j=j, first=first):
                    for t in range(half_x):
                        piece = blocks_ref[first + j, :, t * LANES : (t + 1) * LANES]
                        slots[side, j, pl.ds(t, aux_rows, stride=half_x), :] = piece.astype(jnp.float32)

            weights.append(jnp.transpose(jnp.concatenate(rows, axis=0)).astype(jnp.bfloat16))
        keep = lane < jnp.where(low, sizes_ref[2 * m], sizes_ref[2 * m + 1] + BS)
        for pp in range(aux_rows // 2):
            sums = []
            for side in range(2):
                cols = [
                    jnp.concatenate(
                        [slots[side, j, p * half_x : (p + 1) * half_x, :] for j in range(MOST)], axis=0
                    ).astype(jnp.bfloat16)
                    for p in (2 * pp, 2 * pp + 1)
                ]
                sums.append(
                    jnp.dot(weights[side], jnp.concatenate(cols, axis=1), preferred_element_type=jnp.float32)
                )
            for q in range(2):
                even0 = sums[0][:BS, q * LANES : (q + 1) * LANES]
                odd0 = sums[0][BS:, q * LANES : (q + 1) * LANES]
                even1 = sums[1][:BS, q * LANES : (q + 1) * LANES]
                odd1 = sums[1][BS:, q * LANES : (q + 1) * LANES]
                total = jnp.where(low, even0, odd1) + pltpu.roll(jnp.where(low, even1, odd0), BS, 1)
                turned[pl.ds(2 * pp + q, occ_count, stride=aux_rows), :] = jnp.where(keep, total, 0.0)
        out_ref[:, pl.ds(pl.multiple_of(m * LANES, LANES), LANES)] = turned[...].astype(jnp.bfloat16)
        return carry

    lax.fori_loop(0, block_count // 2, column_pair, 0)


def half_transform(blocks, col_counts, block_sizes, occ_coeff):
    pair_count, aux_rows, _ = blocks.shape
    block_count = col_counts.shape[0]
    occ_count = occ_coeff.shape[1]
    occ = occ_coeff.astype(jnp.float32).reshape(block_count * BS // 2, 2 * occ_count)
    smem = pl.BlockSpec(memory_space=pltpu.SMEM)
    vmem = pl.BlockSpec(memory_space=pltpu.VMEM)
    return pl.pallas_call(
        half_kernel,
        out_shape=jax.ShapeDtypeStruct((occ_count * aux_rows, block_count * BS), jnp.bfloat16),
        in_specs=[smem, smem, vmem, vmem],
        out_specs=vmem,
        scratch_shapes=[
            pltpu.VMEM((2, MOST, aux_rows * BS // 2, LANES), jnp.float32),
            pltpu.VMEM((occ_count * aux_rows, LANES), jnp.float32),
            pltpu.SMEM((block_count,), jnp.int32),
        ],
        compiler_params=pltpu.CompilerParams(vmem_limit_bytes=40 * MIB),
        name="half_transform",
    )(col_counts, block_sizes, occ, blocks)


def response_kernel(weight_ref, half_ref, green_ref, chi_ref, folded, total):
    step = pl.program_id(0)
    sources, own, aux_rows, basis_count = half_ref.shape
    rows = sources * aux_rows
    tile = green_ref.shape[1]

    @pl.when(step == 0)
    def _():
        total[...] = jnp.zeros_like(total)
        for ii in range(own):
            folded[ii] = (
                half_ref[:, ii].astype(jnp.float32).reshape(rows, basis_count) * weight_ref[ii]
            ).astype(jnp.bfloat16)

    columns = pl.ds(pl.multiple_of(step * tile, tile), tile)
    for ii in range(own):
        dressed = jnp.dot(folded[ii], green_ref[...], preferred_element_type=jnp.float32).astype(jnp.bfloat16)
        left = half_ref[:, ii, :, columns].reshape(rows, tile)
        total[...] += lax.dot_general(left, dressed, (((1,), (1,)), ((), ())), preferred_element_type=jnp.float32)

    @pl.when(step == pl.num_programs(0) - 1)
    def _():
        chi_ref[...] = total[...].astype(chi_ref.dtype)


def response(half, weight, virt_green, tile=256):
    sources, own, aux_rows, basis_count = half.shape
    rows = sources * aux_rows
    return pl.pallas_call(
        response_kernel,
        grid=(basis_count // tile,),
        out_shape=jax.ShapeDtypeStruct((rows, rows), jnp.bfloat16),
        in_specs=[
            pl.BlockSpec(memory_space=pltpu.SMEM),
            pl.BlockSpec((sources, own, aux_rows, basis_count), lambda n: (0, 0, 0, 0)),
            pl.BlockSpec((basis_count, tile), lambda n: (0, n)),
        ],
        out_specs=pl.BlockSpec((rows, rows), lambda n: (0, 0)),
        scratch_shapes=[
            pltpu.VMEM((own, rows, basis_count), jnp.bfloat16),
            pltpu.VMEM((rows, rows), jnp.float32),
        ],
        compiler_params=pltpu.CompilerParams(vmem_limit_bytes=40 * MIB),
        name="response",
    )(weight, half, virt_green)


def per_device(blocks, col_counts, block_sizes, occ_coeff, occ_weight, virt_green):
    devices = lax.axis_size("ten")
    _, aux_rows, _ = blocks.shape
    occ_count = occ_coeff.shape[1]
    own = occ_count // devices
    basis_count = devices * BS
    half = half_transform(blocks, col_counts, block_sizes, occ_coeff)
    half = half.reshape(devices, own, aux_rows, basis_count)
    got = lax.all_to_all(half, "ten", split_axis=0, concat_axis=0, tiled=True)
    weight = lax.dynamic_slice(occ_weight, (lax.axis_index("ten") * own,), (own,))
    terms = response(got, weight, virt_green).reshape(devices, aux_rows, devices * aux_rows)
    terms = lax.all_to_all(terms, "ten", split_axis=0, concat_axis=0, tiled=True)
    share = jnp.sum(terms.astype(jnp.float32), axis=0)
    return lax.psum(share, "rep")


def solution(mesh):
    return jax.shard_map(
        per_device,
        mesh=mesh,
        in_specs=(P(None, "ten", None), P(), P(), P(None, "rep"), P("rep"), P()),
        out_specs=P("ten", None),
        check_vma=False,
    )
```

```python
import functools

import jax
import jax.numpy as jnp
from jax import lax
from jax.experimental import pallas as pl
from jax.experimental.pallas import tpu as pltpu
from jax.sharding import PartitionSpec as P

BS = 64
MOST = 4
LANES = 128
MIB = 1024 * 1024
BUFFERS = 3
CHUNKS = (6, 10)


def half_kernel(
    first_pair, pairs, counts_ref, sizes_ref, occ_ref, blocks_ref, out_ref, held, slots, turned, starts, sems
):
    block_count = counts_ref.shape[0]
    pair_count, aux_rows, _ = blocks_ref.shape
    occ_count = BS
    half_x = BS // 2
    pitch = half_x + 1
    turned_pitch = aux_rows + 1
    window = 2 * MOST

    def count_up(b, total):
        starts[b] = total
        return total + counts_ref[b]

    lax.fori_loop(0, 2 * (first_pair + pairs), count_up, jnp.int32(0))

    def base_of(m):
        return jnp.minimum(starts[2 * (first_pair + m)], pair_count - window)

    def fetch(m):
        slot = lax.rem(m, BUFFERS)
        return pltpu.make_async_copy(blocks_ref.at[pl.ds(base_of(m), window)], held.at[slot], sems.at[slot])

    for m in range(min(BUFFERS - 1, pairs)):
        fetch(jnp.int32(m)).start()
    slots[...] = jnp.zeros_like(slots)

    x_of = 2 * lax.broadcasted_iota(jnp.int32, (half_x, LANES), 0) + (
        lax.broadcasted_iota(jnp.int32, (half_x, LANES), 1) // BS
    )
    lane = lax.broadcasted_iota(jnp.int32, (BS, LANES), 1)
    low = lane < BS

    def column_pair(m, carry):
        @pl.when(m + BUFFERS - 1 < pairs)
        def _():
            fetch(m + BUFFERS - 1).start()

        fetch(m).wait()
        slot = lax.rem(m, BUFFERS)
        base = base_of(m)
        weights = []
        for side in range(2):
            b = 2 * (first_pair + m) + side
            first, count = starts[b] - base, counts_ref[b]
            rows = []
            for j in range(MOST):
                offset = (j + 1) // 2 if j % 2 == 1 else -(j // 2)
                row = lax.rem(b + offset + block_count, block_count)
                size = jnp.where(j < count, sizes_ref[row], 0)
                coeff = occ_ref[pl.ds(row * half_x, half_x), :]
                rows.append(jnp.where(x_of < size, coeff, 0.0))

                @pl.when(j < count)
                def _(side=side, j=j, first=first):
                    for t in range(half_x):
                        piece = held[slot, first + j, :, t * LANES : (t + 1) * LANES]
                        slots[side, j, pl.ds(t, aux_rows, stride=pitch), :] = piece.astype(jnp.float32)

            weights.append(jnp.transpose(jnp.concatenate(rows, axis=0)).astype(jnp.bfloat16))
        b = 2 * (first_pair + m)
        keep = lane < jnp.where(low, sizes_ref[b], sizes_ref[b + 1] + BS)
        for pp in range(aux_rows // 2):
            sums = []
            for side in range(2):
                cols = [
                    jnp.concatenate(
                        [slots[side, j, p * pitch : p * pitch + half_x, :] for j in range(MOST)], axis=0
                    ).astype(jnp.bfloat16)
                    for p in (2 * pp, 2 * pp + 1)
                ]
                sums.append(
                    jnp.dot(weights[side], jnp.concatenate(cols, axis=1), preferred_element_type=jnp.float32)
                )
            for q in range(2):
                even0 = sums[0][:BS, q * LANES : (q + 1) * LANES]
                odd0 = sums[0][BS:, q * LANES : (q + 1) * LANES]
                even1 = sums[1][:BS, q * LANES : (q + 1) * LANES]
                odd1 = sums[1][BS:, q * LANES : (q + 1) * LANES]
                total = jnp.where(low, even0, odd1) + pltpu.roll(jnp.where(low, even1, odd0), BS, 1)
                turned[pl.ds(2 * pp + q, occ_count, stride=turned_pitch), :] = jnp.where(keep, total, 0.0)
        for i in range(occ_count):
            out_ref[i * aux_rows : (i + 1) * aux_rows, pl.ds(pl.multiple_of(m * LANES, LANES), LANES)] = turned[
                i * turned_pitch : i * turned_pitch + aux_rows, :
            ].astype(jnp.bfloat16)
        return carry

    lax.fori_loop(0, pairs, column_pair, 0)


def half_transform(blocks, col_counts, block_sizes, occ, first_pair, pairs):
    pair_count, aux_rows, flat = blocks.shape
    block_count = col_counts.shape[0]
    occ_count = occ.shape[1] // 2
    smem = pl.BlockSpec(memory_space=pltpu.SMEM)
    vmem = pl.BlockSpec(memory_space=pltpu.VMEM)
    return pl.pallas_call(
        functools.partial(half_kernel, first_pair, pairs),
        out_shape=jax.ShapeDtypeStruct((occ_count * aux_rows, pairs * LANES), jnp.bfloat16),
        in_specs=[smem, smem, vmem, pl.BlockSpec(memory_space=pltpu.HBM)],
        out_specs=vmem,
        scratch_shapes=[
            pltpu.VMEM((BUFFERS, 2 * MOST, aux_rows, flat), jnp.bfloat16),
            pltpu.VMEM((2, MOST, aux_rows * (BS // 2 + 1), LANES), jnp.float32),
            pltpu.VMEM((occ_count * (aux_rows + 1), LANES), jnp.float32),
            pltpu.SMEM((block_count,), jnp.int32),
            pltpu.SemaphoreType.DMA((BUFFERS,)),
        ],
        compiler_params=pltpu.CompilerParams(vmem_limit_bytes=60 * MIB),
        cost_estimate=pl.CostEstimate(flops=pairs * 10**9, bytes_accessed=pairs * MIB, transcendentals=0),
        name="half_transform",
    )(col_counts, block_sizes, occ, blocks)


def dress_kernel(half_ref, green_ref, out_ref):
    sources, own, aux_rows, depth = half_ref.shape
    rows = sources * aux_rows
    for ii in range(own):
        out_ref[ii] = jnp.dot(
            half_ref[:, ii].reshape(rows, depth), green_ref[...], preferred_element_type=jnp.float32
        )


def dress(half, virt_green, first, tile=256):
    sources, own, aux_rows, depth = half.shape
    rows = sources * aux_rows
    basis_count = virt_green.shape[1]
    return pl.pallas_call(
        dress_kernel,
        grid=(basis_count // tile,),
        out_shape=jax.ShapeDtypeStruct((own, rows, basis_count), jnp.float32),
        in_specs=[
            pl.BlockSpec((sources, own, aux_rows, depth), lambda n: (0, 0, 0, 0)),
            pl.BlockSpec((pl.Element(depth), pl.Element(tile)), lambda n: (first, n * tile)),
        ],
        out_specs=pl.BlockSpec((own, rows, tile), lambda n: (0, 0, n)),
        compiler_params=pltpu.CompilerParams(vmem_limit_bytes=60 * MIB),
        cost_estimate=pl.CostEstimate(
            flops=2 * own * rows * depth * basis_count,
            bytes_accessed=2 * own * rows * depth + 2 * depth * basis_count + 4 * own * rows * basis_count,
            transcendentals=0,
        ),
        name="dress",
    )(half, virt_green)


def response_kernel(split, weight_ref, half0_ref, half1_ref, green_ref, part_ref, chi_ref, total):
    step = pl.program_id(0)
    sources, own, aux_rows, depth = half1_ref.shape
    rows = sources * aux_rows
    tile = green_ref.shape[1]

    @pl.when(step == 0)
    def _():
        total[...] = jnp.zeros_like(total)

    def add(half_ref, columns):
        for ii in range(own):
            dressed = part_ref[ii] + jnp.dot(
                half1_ref[:, ii].reshape(rows, depth), green_ref[...], preferred_element_type=jnp.float32
            )
            dressed = (dressed * weight_ref[ii]).astype(jnp.bfloat16)
            left = half_ref[:, ii, :, columns].reshape(rows, tile)
            total[...] += lax.dot_general(
                left, dressed, (((1,), (1,)), ((), ())), preferred_element_type=jnp.float32
            )

    @pl.when(step < split)
    def _():
        add(half0_ref, pl.ds(pl.multiple_of(step * tile, tile), tile))

    @pl.when(step >= split)
    def _():
        add(half1_ref, pl.ds(pl.multiple_of((step - split) * tile, tile), tile))

    @pl.when(step == pl.num_programs(0) - 1)
    def _():
        chi_ref[...] = total[...].astype(chi_ref.dtype)


def response(half0, half1, weight, part, virt_green, tile=256):
    sources, own, aux_rows, depth0 = half0.shape
    depth1 = half1.shape[3]
    rows = sources * aux_rows
    basis_count = virt_green.shape[1]
    whole = lambda n: (0, 0, 0, 0)
    return pl.pallas_call(
        functools.partial(response_kernel, depth0 // tile),
        grid=(basis_count // tile,),
        out_shape=jax.ShapeDtypeStruct((rows, rows), jnp.bfloat16),
        in_specs=[
            pl.BlockSpec(memory_space=pltpu.SMEM),
            pl.BlockSpec((sources, own, aux_rows, depth0), whole),
            pl.BlockSpec((sources, own, aux_rows, depth1), whole),
            pl.BlockSpec((pl.Element(depth1), pl.Element(tile)), lambda n: (depth0, n * tile)),
            pl.BlockSpec((own, rows, tile), lambda n: (0, 0, n)),
        ],
        out_specs=pl.BlockSpec((rows, rows), lambda n: (0, 0)),
        scratch_shapes=[pltpu.VMEM((rows, rows), jnp.float32)],
        compiler_params=pltpu.CompilerParams(vmem_limit_bytes=60 * MIB),
        name="response",
    )(weight, half0, half1, virt_green, part)


def per_device(blocks, col_counts, block_sizes, occ_coeff, occ_weight, virt_green):
    devices = lax.axis_size("ten")
    aux_rows = blocks.shape[1]
    occ_count = occ_coeff.shape[1]
    own = occ_count // devices
    occ = occ_coeff.astype(jnp.float32).reshape(devices * BS // 2, 2 * occ_count)
    got, first = [], 0
    for pairs in CHUNKS:
        half = half_transform(blocks, col_counts, block_sizes, occ, first, pairs)
        half = half.reshape(devices, own, aux_rows, pairs * LANES)
        got.append(lax.all_to_all(half, "ten", split_axis=0, concat_axis=0, tiled=True))
        first += pairs
    weight = lax.dynamic_slice(occ_weight, (lax.axis_index("ten") * own,), (own,))
    part = dress(got[0], virt_green, 0)
    terms = response(got[0], got[1], weight, part, virt_green).reshape(devices, aux_rows, devices * aux_rows)
    terms = lax.all_to_all(terms, "ten", split_axis=0, concat_axis=0, tiled=True)
    share = jnp.sum(terms.astype(jnp.float32), axis=0)
    groups = lax.axis_size("rep")
    one, two, three = (
        lax.ppermute(share, "rep", [(z, (z + step) % groups) for z in range(groups)]) for step in (1, 2, 3)
    )
    return (share + two) + (one + three)


def solution(mesh):
    return jax.shard_map(
        per_device,
        mesh=mesh,
        in_specs=(P(None, "ten", None), P(), P(), P(None, "rep"), P("rep"), P()),
        out_specs=P("ten", None),
        check_vma=False,
    )
```

```python
import functools

import jax
import jax.numpy as jnp
from jax import lax
from jax.experimental import pallas as pl
from jax.experimental.pallas import tpu as pltpu
from jax.sharding import PartitionSpec as P

BS = 64
MOST = 4
LANES = 128
MIB = 1024 * 1024
BUFFERS = 3
WIDTHS = (12, 13, 14, 16)
FIRST = 4


def prefix_sums(counts_ref, into):
    def count_up(b, total):
        into[b] = total
        return total + counts_ref[b]

    return lax.fori_loop(0, counts_ref.shape[0], count_up, jnp.int32(0))


def targets(position, sizes_ref, offsets, m):
    size0, size1 = sizes_ref[2 * m], sizes_ref[2 * m + 1]
    start = offsets[2 * m]
    second = position >= BS
    local = jnp.where(second, position - BS, position)
    place = (local + jnp.where(second, start + size0, start)) & (LANES - 1)
    return jnp.where(local < jnp.where(second, size1, size0), place, -1)


def half_kernel(
    lo, hi, counts_ref, sizes_ref, occ_ref, blocks_ref, out_ref,
    held, slots, turned, carry, starts, offsets, sems,
):
    block_count = counts_ref.shape[0]
    pair_count, aux_rows, _ = blocks_ref.shape
    occ_count = occ_ref.shape[1]
    half_x = BS // 2
    pitch = half_x + 1
    turned_pitch = aux_rows + 1
    window = 2 * MOST
    last_pair = block_count // 2

    prefix_sums(counts_ref, starts)
    used = prefix_sums(sizes_ref, offsets)

    def count_before(limit):
        return lax.fori_loop(
            0, last_pair, lambda m, n: n + (offsets[2 * m] < limit).astype(jnp.int32), jnp.int32(0)
        )

    m_lo = jnp.int32(0) if lo == 0 else count_before(lo * LANES + 1) - 1
    m_hi = count_before(hi * LANES)

    def base_of(m):
        return jnp.minimum(starts[2 * m], pair_count - window)

    def fetch(m):
        slot = lax.rem(m, BUFFERS)
        return pltpu.make_async_copy(blocks_ref.at[pl.ds(base_of(m), window)], held.at[slot], sems.at[slot])

    for ahead in range(BUFFERS - 1):

        @pl.when(m_lo + ahead < m_hi)
        def _(ahead=ahead):
            fetch(m_lo + ahead).start()

    slots[...] = jnp.zeros_like(slots)
    carry[...] = jnp.zeros_like(carry)

    twice = 2 * lax.broadcasted_iota(jnp.int32, (half_x, occ_count), 0)
    low = lax.broadcasted_iota(jnp.int32, (BS, LANES), 1) < BS
    square_row = lax.broadcasted_iota(jnp.int32, (LANES, LANES), 0)
    square_lane = lax.broadcasted_iota(jnp.int32, (LANES, LANES), 1)

    def column_pair(m, state):
        @pl.when(m + BUFFERS - 1 < m_hi)
        def _():
            fetch(m + BUFFERS - 1).start()

        fetch(m).wait()
        slot = lax.rem(m, BUFFERS)
        base = base_of(m)
        weights = []
        for side in range(2):
            b = 2 * m + side
            first, count = starts[b] - base, counts_ref[b]
            rows = [[], []]
            for j in range(MOST):
                offset = (j + 1) // 2 if j % 2 == 1 else -(j // 2)
                row = lax.rem(b + offset + block_count, block_count)
                size = jnp.where(j < count, sizes_ref[row], 0)
                for parity in range(2):
                    coeff = occ_ref[pl.ds(row * BS + parity, half_x, stride=2), :]
                    rows[parity].append(jnp.where(twice + parity < size, coeff, 0.0))

                @pl.when(j < count)
                def _(side=side, j=j, first=first):
                    for t in range(half_x):
                        piece = held[slot, first + j, :, t * LANES : (t + 1) * LANES]
                        slots[side, j, pl.ds(t, aux_rows, stride=pitch), :] = piece.astype(jnp.float32)

            weights.append(
                jnp.concatenate(
                    [jnp.transpose(jnp.concatenate(part, axis=0)) for part in rows], axis=0
                ).astype(jnp.bfloat16)
            )
        for pp in range(aux_rows // 2):
            sums = []
            for side in range(2):
                cols = [
                    jnp.concatenate(
                        [slots[side, j, p * pitch : p * pitch + half_x, :] for j in range(MOST)], axis=0
                    ).astype(jnp.bfloat16)
                    for p in (2 * pp, 2 * pp + 1)
                ]
                sums.append(
                    jnp.dot(weights[side], jnp.concatenate(cols, axis=1), preferred_element_type=jnp.float32)
                )
            for q in range(2):
                even0 = sums[0][:BS, q * LANES : (q + 1) * LANES]
                odd0 = sums[0][BS:, q * LANES : (q + 1) * LANES]
                even1 = sums[1][:BS, q * LANES : (q + 1) * LANES]
                odd1 = sums[1][BS:, q * LANES : (q + 1) * LANES]
                turned[pl.ds(2 * pp + q, occ_count, stride=turned_pitch), :] = jnp.where(
                    low, even0, odd1
                ) + pltpu.roll(jnp.where(low, even1, odd0), BS, 1)

        start = offsets[2 * m]
        tile, split = start // LANES, start % LANES
        filled = split + sizes_ref[2 * m] + sizes_ref[2 * m + 1]
        full = filled >= LANES
        select = (square_lane == targets(square_row, sizes_ref, offsets, m)).astype(jnp.bfloat16)
        here = square_lane >= split
        column = pl.ds(pl.multiple_of(jnp.maximum(tile - lo, 0) * LANES, LANES), LANES)
        group = LANES // aux_rows
        for g in range(occ_count // group):
            values = jnp.concatenate(
                [turned[i * turned_pitch : i * turned_pitch + aux_rows, :] for i in range(g * group, (g + 1) * group)],
                axis=0,
            ).astype(jnp.bfloat16)
            moved = jnp.dot(values, select, preferred_element_type=jnp.float32)
            rows = slice(g * LANES, (g + 1) * LANES)
            current = carry[rows, :] + jnp.where(here, moved, 0.0)
            out_ref[rows, column] = current.astype(jnp.bfloat16)
            carry[rows, :] = jnp.where(full, jnp.where(here, 0.0, moved), current)
        return jnp.where(filled > LANES, tile + 1, -1)

    spill = lax.fori_loop(m_lo, m_hi, column_pair, jnp.int32(-1))

    def zero(tile, state):
        out_ref[:, pl.ds(pl.multiple_of((tile - lo) * LANES, LANES), LANES)] = jnp.zeros(
            (out_ref.shape[0], LANES), jnp.bfloat16
        )
        return state

    lax.fori_loop(jnp.maximum((used + LANES - 1) // LANES, lo), hi, zero, 0)

    @pl.when((spill >= lo) & (spill < hi))
    def _():
        out_ref[:, pl.ds(pl.multiple_of((spill - lo) * LANES, LANES), LANES)] = carry[...].astype(jnp.bfloat16)


def half_transform(blocks, col_counts, block_sizes, occ, lo, hi):
    pair_count, aux_rows, flat = blocks.shape
    block_count = col_counts.shape[0]
    occ_count = occ.shape[1]
    smem = pl.BlockSpec(memory_space=pltpu.SMEM)
    vmem = pl.BlockSpec(memory_space=pltpu.VMEM)
    return pl.pallas_call(
        functools.partial(half_kernel, lo, hi),
        out_shape=jax.ShapeDtypeStruct((occ_count * aux_rows, (hi - lo) * LANES), jnp.bfloat16),
        in_specs=[smem, smem, vmem, pl.BlockSpec(memory_space=pltpu.HBM)],
        out_specs=vmem,
        scratch_shapes=[
            pltpu.VMEM((BUFFERS, 2 * MOST, aux_rows, flat), jnp.bfloat16),
            pltpu.VMEM((2, MOST, aux_rows * (BS // 2 + 1), LANES), jnp.float32),
            pltpu.VMEM((occ_count * (aux_rows + 1), LANES), jnp.float32),
            pltpu.VMEM((occ_count * aux_rows, LANES), jnp.float32),
            pltpu.SMEM((block_count,), jnp.int32),
            pltpu.SMEM((block_count,), jnp.int32),
            pltpu.SemaphoreType.DMA((BUFFERS,)),
        ],
        compiler_params=pltpu.CompilerParams(vmem_limit_bytes=60 * MIB),
        cost_estimate=pl.CostEstimate(flops=(hi - lo) * 10**9, bytes_accessed=(hi - lo) * MIB, transcendentals=0),
        name="half_transform",
    )(col_counts, block_sizes, occ, blocks)


def pack_kernel(sizes_ref, green_ref, out_ref, packed_rows, row_carry, lane_carry, offsets):
    basis_count = green_ref.shape[0]
    width = out_ref.shape[0]
    last_pair = sizes_ref.shape[0] // 2
    used = prefix_sums(sizes_ref, offsets)
    tiles = (used + LANES - 1) // LANES
    square_row = lax.broadcasted_iota(jnp.int32, (LANES, LANES), 0)
    square_lane = lax.broadcasted_iota(jnp.int32, (LANES, LANES), 1)
    strip = 4 * LANES
    row_carry[...] = jnp.zeros_like(row_carry)
    lane_carry[...] = jnp.zeros_like(lane_carry)

    def place(m):
        start = offsets[2 * m]
        split = start % LANES
        return start // LANES, split, split + sizes_ref[2 * m] + sizes_ref[2 * m + 1]

    def at(tile):
        return pl.ds(pl.multiple_of(tile * LANES, LANES), LANES)

    def pack_rows(m, state):
        tile, split, filled = place(m)
        select = (square_row == targets(square_lane, sizes_ref, offsets, m)).astype(jnp.bfloat16)
        here = lax.broadcasted_iota(jnp.int32, (LANES, strip), 0) >= split
        for s in range(basis_count // strip):
            lanes = slice(s * strip, (s + 1) * strip)
            moved = jnp.dot(select, green_ref[at(m), lanes], preferred_element_type=jnp.float32)
            current = row_carry[:, lanes] + jnp.where(here, moved, 0.0)
            packed_rows[at(tile), lanes] = current.astype(jnp.bfloat16)
            row_carry[:, lanes] = jnp.where(filled >= LANES, jnp.where(here, 0.0, moved), current)
        return jnp.where(filled > LANES, tile + 1, -1)

    spill = lax.fori_loop(0, last_pair, pack_rows, jnp.int32(-1))

    def zero_rows(tile, state):
        packed_rows[at(tile), :] = jnp.zeros((LANES, basis_count), jnp.bfloat16)
        return state

    lax.fori_loop(tiles, width // LANES, zero_rows, 0)

    @pl.when(spill >= 0)
    def _():
        packed_rows[at(spill), :] = row_carry[...].astype(jnp.bfloat16)

    def pack_lanes(m, state):
        tile, split, filled = place(m)
        select = (square_lane == targets(square_row, sizes_ref, offsets, m)).astype(jnp.bfloat16)
        here = square_lane >= split
        for r in range(width // LANES):
            rows = slice(r * LANES, (r + 1) * LANES)
            moved = jnp.dot(packed_rows[rows, at(m)], select, preferred_element_type=jnp.float32)
            current = lane_carry[rows, :] + jnp.where(here, moved, 0.0)
            out_ref[rows, at(tile)] = current.astype(jnp.bfloat16)
            lane_carry[rows, :] = jnp.where(filled >= LANES, jnp.where(here, 0.0, moved), current)
        return state

    lax.fori_loop(0, last_pair, pack_lanes, 0)

    def zero_lanes(tile, state):
        out_ref[:, at(tile)] = jnp.zeros((width, LANES), jnp.bfloat16)
        return state

    lax.fori_loop(tiles, width // LANES, zero_lanes, 0)

    @pl.when(spill >= 0)
    def _():
        out_ref[:, at(spill)] = lane_carry[...].astype(jnp.bfloat16)


def pack_green(block_sizes, virt_green, width):
    basis_count = virt_green.shape[0]
    vmem = pl.BlockSpec(memory_space=pltpu.VMEM)
    return pl.pallas_call(
        pack_kernel,
        out_shape=jax.ShapeDtypeStruct((width, width), jnp.bfloat16),
        in_specs=[pl.BlockSpec(memory_space=pltpu.SMEM), vmem],
        out_specs=vmem,
        scratch_shapes=[
            pltpu.VMEM((width, basis_count), jnp.bfloat16),
            pltpu.VMEM((LANES, basis_count), jnp.float32),
            pltpu.VMEM((width, LANES), jnp.float32),
            pltpu.SMEM((block_sizes.shape[0],), jnp.int32),
        ],
        compiler_params=pltpu.CompilerParams(vmem_limit_bytes=60 * MIB),
        cost_estimate=pl.CostEstimate(flops=10 * 10**9, bytes_accessed=14 * MIB, transcendentals=0),
        name="pack_green",
    )(block_sizes, virt_green)


def dress_kernel(half_ref, green_ref, out_ref):
    sources, own, aux_rows, depth = half_ref.shape
    rows = sources * aux_rows
    for ii in range(own):
        out_ref[ii] = jnp.dot(
            half_ref[:, ii].reshape(rows, depth), green_ref[...], preferred_element_type=jnp.float32
        )


def column_start(step, tile, width):
    return pl.multiple_of(jnp.minimum(step * tile, width - tile), LANES)


def dress(half, green, tile=256):
    sources, own, aux_rows, depth = half.shape
    rows = sources * aux_rows
    width = green.shape[1]
    steps = pl.cdiv(width, tile)
    return pl.pallas_call(
        dress_kernel,
        grid=(steps,),
        out_shape=jax.ShapeDtypeStruct((own, rows, steps * tile), jnp.float32),
        in_specs=[
            pl.BlockSpec((sources, own, aux_rows, depth), lambda n: (0, 0, 0, 0)),
            pl.BlockSpec((pl.Element(depth), pl.Element(tile)), lambda n: (0, column_start(n, tile, width))),
        ],
        out_specs=pl.BlockSpec((own, rows, tile), lambda n: (0, 0, n)),
        compiler_params=pltpu.CompilerParams(vmem_limit_bytes=60 * MIB),
        cost_estimate=pl.CostEstimate(
            flops=2 * own * rows * depth * width,
            bytes_accessed=2 * own * rows * depth + 2 * depth * width + 4 * own * rows * width,
            transcendentals=0,
        ),
        name="dress",
    )(half, green)


def response_kernel(split, width, weight_ref, half0_ref, half1_ref, green_ref, part_ref, chi_ref, total):
    step = pl.program_id(0)
    sources, own, aux_rows, depth = half1_ref.shape
    rows = sources * aux_rows
    tile = green_ref.shape[1]
    start = column_start(step, tile, width)
    fresh = lax.broadcasted_iota(jnp.int32, (rows, tile), 1) >= step * tile - start

    @pl.when(step == 0)
    def _():
        total[...] = jnp.zeros_like(total)

    def add(half_ref, first):
        columns = pl.ds(pl.multiple_of(start - first, LANES), tile)
        for ii in range(own):
            dressed = part_ref[ii] + jnp.dot(
                half1_ref[:, ii].reshape(rows, depth), green_ref[...], preferred_element_type=jnp.float32
            )
            dressed = jnp.where(fresh, dressed * weight_ref[ii], 0.0).astype(jnp.bfloat16)
            left = half_ref[:, ii, :, columns].reshape(rows, tile)
            total[...] += lax.dot_general(
                left, dressed, (((1,), (1,)), ((), ())), preferred_element_type=jnp.float32
            )

    @pl.when(step < split // tile)
    def _():
        add(half0_ref, 0)

    @pl.when(step >= split // tile)
    def _():
        add(half1_ref, split)

    @pl.when(step == pl.num_programs(0) - 1)
    def _():
        chi_ref[...] = total[...].astype(chi_ref.dtype)


def response(half0, half1, weight, part, green, tile=256):
    sources, own, aux_rows, depth0 = half0.shape
    depth1 = half1.shape[3]
    rows = sources * aux_rows
    width = depth0 + depth1
    whole = lambda n: (0, 0, 0, 0)
    return pl.pallas_call(
        functools.partial(response_kernel, depth0, width),
        grid=(pl.cdiv(width, tile),),
        out_shape=jax.ShapeDtypeStruct((rows, rows), jnp.bfloat16),
        in_specs=[
            pl.BlockSpec(memory_space=pltpu.SMEM),
            pl.BlockSpec((sources, own, aux_rows, depth0), whole),
            pl.BlockSpec((sources, own, aux_rows, depth1), whole),
            pl.BlockSpec((pl.Element(depth1), pl.Element(tile)), lambda n: (depth0, column_start(n, tile, width))),
            pl.BlockSpec((own, rows, tile), lambda n: (0, 0, n)),
        ],
        out_specs=pl.BlockSpec((rows, rows), lambda n: (0, 0)),
        scratch_shapes=[pltpu.VMEM((rows, rows), jnp.float32)],
        compiler_params=pltpu.CompilerParams(vmem_limit_bytes=60 * MIB),
        name="response",
    )(weight, half0, half1, green, part)


def chi_terms(tiles, blocks, col_counts, block_sizes, occ, weight, virt_green):
    devices = lax.axis_size("ten")
    aux_rows = blocks.shape[1]
    own = weight.shape[0]
    got = []
    for lo, hi in ((0, FIRST), (FIRST, tiles)):
        half = half_transform(blocks, col_counts, block_sizes, occ, lo, hi)
        half = half.reshape(devices, own, aux_rows, (hi - lo) * LANES)
        got.append(lax.all_to_all(half, "ten", split_axis=0, concat_axis=0, tiled=True))
    green = pack_green(block_sizes, virt_green, tiles * LANES)
    part = dress(got[0], green)
    return response(got[0], got[1], weight, part, green)


def per_device(blocks, col_counts, block_sizes, occ_coeff, occ_weight, virt_green):
    devices = lax.axis_size("ten")
    aux_rows = blocks.shape[1]
    own = occ_coeff.shape[1] // devices
    occ = occ_coeff.astype(jnp.float32)
    weight = lax.dynamic_slice(occ_weight, (lax.axis_index("ten") * own,), (own,))
    used = jnp.sum(block_sizes)
    case = sum((used > tiles * LANES).astype(jnp.int32) for tiles in WIDTHS[:-1])
    terms = lax.switch(
        case,
        [functools.partial(chi_terms, tiles) for tiles in WIDTHS],
        blocks, col_counts, block_sizes, occ, weight, virt_green,
    )
    terms = terms.reshape(devices, aux_rows, devices * aux_rows)
    terms = lax.all_to_all(terms, "ten", split_axis=0, concat_axis=0, tiled=True)
    share = jnp.sum(terms.astype(jnp.float32), axis=0)
    groups = lax.axis_size("rep")
    one, two, three = (
        lax.ppermute(share, "rep", [(z, (z + step) % groups) for z in range(groups)]) for step in (1, 2, 3)
    )
    return (share + two) + (one + three)


def solution(mesh):
    return jax.shard_map(
        per_device,
        mesh=mesh,
        in_specs=(P(None, "ten", None), P(), P(), P(None, "rep"), P("rep"), P()),
        out_specs=P("ten", None),
        check_vma=False,
    )
```

```python
import functools

import jax
import jax.numpy as jnp
from jax import lax
from jax.experimental import pallas as pl
from jax.experimental.pallas import tpu as pltpu
from jax.sharding import PartitionSpec as P

BS = 64
MOST = 4
LANES = 128
MIB = 1024 * 1024
BUFFERS = 4
WIDTHS = (12, 13, 16)
FIRST = 4


def prefix_sums(counts_ref, into):
    total = jnp.int32(0)
    for b in range(counts_ref.shape[0]):
        into[b] = total
        total = total + counts_ref[b]
    return total


def targets(position, sizes_ref, offsets, m):
    size0, size1 = sizes_ref[2 * m], sizes_ref[2 * m + 1]
    start = offsets[2 * m]
    second = position >= BS
    local = jnp.where(second, position - BS, position)
    place = (local + jnp.where(second, start + size0, start)) & (LANES - 1)
    return jnp.where(local < jnp.where(second, size1, size0), place, -1)


def half_kernel(lo, his, counts_ref, sizes_ref, occ_ref, blocks_ref, *refs):
    outs = refs[: len(his)]
    held, slots, turned, weights, carry, stage, starts, offsets, sems, out_sem = refs[len(his) :]
    block_count = counts_ref.shape[0]
    pair_count, aux_rows, _ = blocks_ref.shape
    occ_count = occ_ref.shape[1]
    half_x = BS // 2
    pitch = half_x + 1
    turned_pitch = aux_rows + 1
    window = 2 * MOST
    last_pair = block_count // 2

    prefix_sums(counts_ref, starts)
    used = prefix_sums(sizes_ref, offsets)
    hi = jnp.int32(his[-1])
    for smaller in reversed(his[:-1]):
        hi = jnp.where(used <= smaller * LANES, smaller, hi)

    def count_before(limit):
        return sum((offsets[2 * m] < limit).astype(jnp.int32) for m in range(last_pair))

    m_lo = jnp.int32(0) if lo == 0 else count_before(lo * LANES + 1) - 1
    m_hi = count_before(hi * LANES)

    def base_of(m):
        return jnp.minimum(starts[2 * m], pair_count - window)

    def fetch(m):
        slot = m & (BUFFERS - 1)
        return pltpu.make_async_copy(blocks_ref.at[pl.ds(base_of(m), window)], held.at[slot], sems.at[slot])

    for ahead in range(BUFFERS - 1):

        @pl.when(m_lo + ahead < m_hi)
        def _(ahead=ahead):
            fetch(m_lo + ahead).start()

    slots[...] = jnp.zeros_like(slots)
    carry[...] = jnp.zeros_like(carry)
    turned[...] = jnp.zeros_like(turned)

    twice = 2 * lax.broadcasted_iota(jnp.int32, (half_x, occ_count), 0)
    low = lax.broadcasted_iota(jnp.int32, (BS, LANES), 1) < BS
    square_row = lax.broadcasted_iota(jnp.int32, (LANES, LANES), 0)
    square_lane = lax.broadcasted_iota(jnp.int32, (LANES, LANES), 1)

    def set_weights(m):
        for side in range(2):
            b = 2 * m + side
            count = counts_ref[b]
            rows = [[], []]
            for j in range(MOST):
                row = b + ((j + 1) // 2 if j % 2 == 1 else -(j // 2))
                row = jnp.where(row < 0, row + block_count, row)
                row = jnp.where(row >= block_count, row - block_count, row)
                size = jnp.where(j < count, sizes_ref[row], 0)
                for parity in range(2):
                    coeff = occ_ref[pl.ds(row * BS + parity, half_x, stride=2), :]
                    rows[parity].append(jnp.where(twice + parity < size, coeff, 0.0))
            for parity in range(2):
                weights[side, parity * occ_count : (parity + 1) * occ_count, :] = jnp.transpose(
                    jnp.concatenate(rows[parity], axis=0)
                ).astype(jnp.bfloat16)

    def turn_blocks(m):
        slot = m & (BUFFERS - 1)
        base = base_of(m)
        for side in range(2):
            first, count = starts[2 * m + side] - base, counts_ref[2 * m + side]
            for j in range(MOST):

                @pl.when(j < count)
                def _(side=side, j=j, first=first):
                    for t in range(half_x):
                        piece = held[slot, first + j, :, t * LANES : (t + 1) * LANES]
                        slots[side, j, pl.ds(t, aux_rows, stride=pitch), :] = piece.astype(jnp.float32)

    def multiply():
        for pp in range(aux_rows // 2):
            sums = []
            for side in range(2):
                cols = [
                    jnp.concatenate(
                        [slots[side, j, p * pitch : p * pitch + half_x, :] for j in range(MOST)], axis=0
                    ).astype(jnp.bfloat16)
                    for p in (2 * pp, 2 * pp + 1)
                ]
                sums.append(
                    jnp.dot(weights[side], jnp.concatenate(cols, axis=1), preferred_element_type=jnp.float32)
                )
            for q in range(2):
                even0 = sums[0][:BS, q * LANES : (q + 1) * LANES]
                odd0 = sums[0][BS:, q * LANES : (q + 1) * LANES]
                even1 = sums[1][:BS, q * LANES : (q + 1) * LANES]
                odd1 = sums[1][BS:, q * LANES : (q + 1) * LANES]
                turned[pl.ds(2 * pp + q, occ_count, stride=turned_pitch), :] = jnp.where(
                    low, even0, odd1
                ) + pltpu.roll(jnp.where(low, even1, odd0), BS, 1)

    def pack(m, valid):
        start = offsets[2 * m]
        tile, split = start >> 7, start & (LANES - 1)
        filled = split + sizes_ref[2 * m] + sizes_ref[2 * m + 1]
        full = valid & (filled >= LANES)
        select = square_lane == jnp.where(valid, targets(square_row, sizes_ref, offsets, m), -1)
        select = select.astype(jnp.bfloat16)
        here = square_lane >= split
        column = pl.ds(pl.multiple_of(jnp.maximum(tile - lo, 0) * LANES, LANES), LANES)
        group = LANES // aux_rows
        for g in range(occ_count // group):
            values = jnp.concatenate(
                [turned[i * turned_pitch : i * turned_pitch + aux_rows, :] for i in range(g * group, (g + 1) * group)],
                axis=0,
            ).astype(jnp.bfloat16)
            moved = jnp.dot(values, select, preferred_element_type=jnp.float32)
            rows = slice(g * LANES, (g + 1) * LANES)
            current = carry[rows, :] + jnp.where(here, moved, 0.0)
            stage[rows, column] = current.astype(jnp.bfloat16)
            carry[rows, :] = jnp.where(full, jnp.where(here, 0.0, moved), current)
        return jnp.where(filled > LANES, tile + 1, -1)

    set_weights(m_lo)

    def column_pair(m, state):
        @pl.when(m + BUFFERS - 1 < m_hi)
        def _():
            fetch(m + BUFFERS - 1).start()

        @pl.when(m < m_hi)
        def _():
            fetch(m).wait()
            turn_blocks(m)

        spill = pack(jnp.maximum(m - 1, m_lo), m > m_lo)
        multiply()
        set_weights(jnp.minimum(m + 1, last_pair - 1))
        return spill

    spill = lax.fori_loop(m_lo, m_hi + 1, column_pair, jnp.int32(-1))

    def zero(tile, state):
        stage[:, pl.ds(pl.multiple_of((tile - lo) * LANES, LANES), LANES)] = jnp.zeros(
            (stage.shape[0], LANES), jnp.bfloat16
        )
        return state

    lax.fori_loop(jnp.maximum((used + LANES - 1) >> 7, lo), hi, zero, 0)

    @pl.when((spill >= lo) & (spill < hi))
    def _():
        stage[:, pl.ds(pl.multiple_of((spill - lo) * LANES, LANES), LANES)] = carry[...].astype(jnp.bfloat16)

    for out_ref, tiles in zip(outs, his):

        @pl.when(hi == tiles)
        def _(out_ref=out_ref, tiles=tiles):
            copy = pltpu.make_async_copy(stage.at[:, : (tiles - lo) * LANES], out_ref, out_sem)
            copy.start()
            copy.wait()


def half_transform(blocks, col_counts, block_sizes, occ, lo, his):
    pair_count, aux_rows, flat = blocks.shape
    block_count = col_counts.shape[0]
    occ_count = occ.shape[1]
    smem = pl.BlockSpec(memory_space=pltpu.SMEM)
    vmem = pl.BlockSpec(memory_space=pltpu.VMEM)
    hbm = pl.BlockSpec(memory_space=pltpu.HBM)
    return pl.pallas_call(
        functools.partial(half_kernel, lo, his),
        out_shape=[jax.ShapeDtypeStruct((occ_count * aux_rows, (hi - lo) * LANES), jnp.bfloat16) for hi in his],
        in_specs=[smem, smem, vmem, hbm],
        out_specs=[hbm] * len(his),
        scratch_shapes=[
            pltpu.VMEM((BUFFERS, 2 * MOST, aux_rows, flat), jnp.bfloat16),
            pltpu.VMEM((2, MOST, aux_rows * (BS // 2 + 1), LANES), jnp.float32),
            pltpu.VMEM((occ_count * (aux_rows + 1), LANES), jnp.float32),
            pltpu.VMEM((2, 2 * occ_count, MOST * BS // 2), jnp.bfloat16),
            pltpu.VMEM((occ_count * aux_rows, LANES), jnp.float32),
            pltpu.VMEM((occ_count * aux_rows, (his[-1] - lo) * LANES), jnp.bfloat16),
            pltpu.SMEM((block_count,), jnp.int32),
            pltpu.SMEM((block_count,), jnp.int32),
            pltpu.SemaphoreType.DMA((BUFFERS,)),
            pltpu.SemaphoreType.DMA,
        ],
        compiler_params=pltpu.CompilerParams(vmem_limit_bytes=60 * MIB),
        cost_estimate=pl.CostEstimate(flops=8 * 10**9, bytes_accessed=8 * MIB, transcendentals=0),
        name="half_transform",
    )(col_counts, block_sizes, occ, blocks)


def pack_kernel(sizes_ref, green_ref, out_ref, packed_rows, row_carry, lane_carry, offsets):
    basis_count = green_ref.shape[0]
    width = out_ref.shape[0]
    last_pair = sizes_ref.shape[0] // 2
    used = prefix_sums(sizes_ref, offsets)
    tiles = (used + LANES - 1) >> 7
    square_row = lax.broadcasted_iota(jnp.int32, (LANES, LANES), 0)
    square_lane = lax.broadcasted_iota(jnp.int32, (LANES, LANES), 1)
    strip = 4 * LANES
    row_carry[...] = jnp.zeros_like(row_carry)
    lane_carry[...] = jnp.zeros_like(lane_carry)

    def place(m):
        start = offsets[2 * m]
        split = start & (LANES - 1)
        return start >> 7, split, split + sizes_ref[2 * m] + sizes_ref[2 * m + 1]

    def at(tile):
        return pl.ds(pl.multiple_of(tile * LANES, LANES), LANES)

    def pack_rows(m, state):
        tile, split, filled = place(m)
        select = (square_row == targets(square_lane, sizes_ref, offsets, m)).astype(jnp.bfloat16)
        here = lax.broadcasted_iota(jnp.int32, (LANES, strip), 0) >= split
        for s in range(basis_count // strip):
            lanes = slice(s * strip, (s + 1) * strip)
            moved = jnp.dot(select, green_ref[at(m), lanes], preferred_element_type=jnp.float32)
            current = row_carry[:, lanes] + jnp.where(here, moved, 0.0)
            packed_rows[at(tile), lanes] = current.astype(jnp.bfloat16)
            row_carry[:, lanes] = jnp.where(filled >= LANES, jnp.where(here, 0.0, moved), current)
        return jnp.where(filled > LANES, tile + 1, -1)

    spill = lax.fori_loop(0, last_pair, pack_rows, jnp.int32(-1))

    def zero_rows(tile, state):
        packed_rows[at(tile), :] = jnp.zeros((LANES, basis_count), jnp.bfloat16)
        return state

    lax.fori_loop(tiles, width // LANES, zero_rows, 0)

    @pl.when(spill >= 0)
    def _():
        packed_rows[at(spill), :] = row_carry[...].astype(jnp.bfloat16)

    def pack_lanes(m, state):
        tile, split, filled = place(m)
        select = (square_lane == targets(square_row, sizes_ref, offsets, m)).astype(jnp.bfloat16)
        here = square_lane >= split
        for r in range(width // LANES):
            rows = slice(r * LANES, (r + 1) * LANES)
            moved = jnp.dot(packed_rows[rows, at(m)], select, preferred_element_type=jnp.float32)
            current = lane_carry[rows, :] + jnp.where(here, moved, 0.0)
            out_ref[rows, at(tile)] = current.astype(jnp.bfloat16)
            lane_carry[rows, :] = jnp.where(filled >= LANES, jnp.where(here, 0.0, moved), current)
        return state

    lax.fori_loop(0, last_pair, pack_lanes, 0)

    def zero_lanes(tile, state):
        out_ref[:, at(tile)] = jnp.zeros((width, LANES), jnp.bfloat16)
        return state

    lax.fori_loop(tiles, width // LANES, zero_lanes, 0)

    @pl.when(spill >= 0)
    def _():
        out_ref[:, at(spill)] = lane_carry[...].astype(jnp.bfloat16)


def pack_green(block_sizes, virt_green, width):
    basis_count = virt_green.shape[0]
    vmem = pl.BlockSpec(memory_space=pltpu.VMEM)
    return pl.pallas_call(
        pack_kernel,
        out_shape=jax.ShapeDtypeStruct((width, width), jnp.bfloat16),
        in_specs=[pl.BlockSpec(memory_space=pltpu.SMEM), vmem],
        out_specs=vmem,
        scratch_shapes=[
            pltpu.VMEM((width, basis_count), jnp.bfloat16),
            pltpu.VMEM((LANES, basis_count), jnp.float32),
            pltpu.VMEM((width, LANES), jnp.float32),
            pltpu.SMEM((block_sizes.shape[0],), jnp.int32),
        ],
        compiler_params=pltpu.CompilerParams(vmem_limit_bytes=60 * MIB),
        cost_estimate=pl.CostEstimate(flops=10 * 10**9, bytes_accessed=14 * MIB, transcendentals=0),
        name="pack_green",
    )(block_sizes, virt_green)


def dress_kernel(half_ref, green_ref, out_ref):
    sources, own, aux_rows, depth = half_ref.shape
    rows = sources * aux_rows
    for ii in range(own):
        out_ref[ii] = jnp.dot(
            half_ref[:, ii].reshape(rows, depth), green_ref[...], preferred_element_type=jnp.float32
        )


def column_start(step, tile, width):
    return pl.multiple_of(jnp.minimum(step * tile, width - tile), LANES)


def dress(half, green, tile=256):
    sources, own, aux_rows, depth = half.shape
    rows = sources * aux_rows
    width = green.shape[1]
    steps = pl.cdiv(width, tile)
    return pl.pallas_call(
        dress_kernel,
        grid=(steps,),
        out_shape=jax.ShapeDtypeStruct((own, rows, steps * tile), jnp.float32),
        in_specs=[
            pl.BlockSpec((sources, own, aux_rows, depth), lambda n: (0, 0, 0, 0)),
            pl.BlockSpec((pl.Element(depth), pl.Element(tile)), lambda n: (0, column_start(n, tile, width))),
        ],
        out_specs=pl.BlockSpec((own, rows, tile), lambda n: (0, 0, n)),
        compiler_params=pltpu.CompilerParams(vmem_limit_bytes=60 * MIB),
        cost_estimate=pl.CostEstimate(
            flops=2 * own * rows * depth * width,
            bytes_accessed=2 * own * rows * depth + 2 * depth * width + 4 * own * rows * width,
            transcendentals=0,
        ),
        name="dress",
    )(half, green)


def response_kernel(split, width, weight_ref, half0_ref, half1_ref, green_ref, part_ref, chi_ref, total):
    step = pl.program_id(0)
    sources, own, aux_rows, depth = half1_ref.shape
    rows = sources * aux_rows
    tile = green_ref.shape[1]
    start = column_start(step, tile, width)
    fresh = lax.broadcasted_iota(jnp.int32, (rows, tile), 1) >= step * tile - start

    @pl.when(step == 0)
    def _():
        total[...] = jnp.zeros_like(total)

    def add(half_ref, first):
        columns = pl.ds(pl.multiple_of(start - first, LANES), tile)
        for ii in range(own):
            dressed = part_ref[ii] + jnp.dot(
                half1_ref[:, ii].reshape(rows, depth), green_ref[...], preferred_element_type=jnp.float32
            )
            dressed = jnp.where(fresh, dressed * weight_ref[ii], 0.0).astype(jnp.bfloat16)
            left = half_ref[:, ii, :, columns].reshape(rows, tile)
            total[...] += lax.dot_general(
                left, dressed, (((1,), (1,)), ((), ())), preferred_element_type=jnp.float32
            )

    @pl.when(step < split // tile)
    def _():
        add(half0_ref, 0)

    @pl.when(step >= split // tile)
    def _():
        add(half1_ref, split)

    @pl.when(step == pl.num_programs(0) - 1)
    def _():
        chi_ref[...] = total[...].astype(chi_ref.dtype)


def response(half0, half1, weight, part, green, tile=256):
    sources, own, aux_rows, depth0 = half0.shape
    depth1 = half1.shape[3]
    rows = sources * aux_rows
    width = depth0 + depth1
    whole = lambda n: (0, 0, 0, 0)
    return pl.pallas_call(
        functools.partial(response_kernel, depth0, width),
        grid=(pl.cdiv(width, tile),),
        out_shape=jax.ShapeDtypeStruct((rows, rows), jnp.bfloat16),
        in_specs=[
            pl.BlockSpec(memory_space=pltpu.SMEM),
            pl.BlockSpec((sources, own, aux_rows, depth0), whole),
            pl.BlockSpec((sources, own, aux_rows, depth1), whole),
            pl.BlockSpec((pl.Element(depth1), pl.Element(tile)), lambda n: (depth0, column_start(n, tile, width))),
            pl.BlockSpec((own, rows, tile), lambda n: (0, 0, n)),
        ],
        out_specs=pl.BlockSpec((rows, rows), lambda n: (0, 0)),
        scratch_shapes=[pltpu.VMEM((rows, rows), jnp.float32)],
        compiler_params=pltpu.CompilerParams(vmem_limit_bytes=60 * MIB),
        name="response",
    )(weight, half0, half1, green, part)


def finish(tiles, got, halves, block_sizes, weight, virt_green):
    devices, own, aux_rows, _ = got.shape
    half = halves[WIDTHS.index(tiles)].reshape(devices, own, aux_rows, (tiles - FIRST) * LANES)
    rest = lax.all_to_all(half, "ten", split_axis=0, concat_axis=0, tiled=True)
    green = pack_green(block_sizes, virt_green, tiles * LANES)
    part = dress(got, green)
    terms = response(got, rest, weight, part, green).reshape(devices, aux_rows, devices * aux_rows)
    terms = lax.all_to_all(terms, "ten", split_axis=0, concat_axis=0, tiled=True)
    share = jnp.sum(terms.astype(jnp.float32), axis=0)
    groups = lax.axis_size("rep")
    one, two, three = (
        lax.ppermute(share, "rep", [(z, (z + step) % groups) for z in range(groups)]) for step in (1, 2, 3)
    )
    return (share + two) + (one + three)


def per_device(blocks, col_counts, block_sizes, occ_coeff, occ_weight, virt_green):
    devices = lax.axis_size("ten")
    aux_rows = blocks.shape[1]
    own = occ_coeff.shape[1] // devices
    occ = occ_coeff.astype(jnp.float32)
    (half,) = half_transform(blocks, col_counts, block_sizes, occ, 0, (FIRST,))
    half = half.reshape(devices, own, aux_rows, FIRST * LANES)
    got = lax.all_to_all(half, "ten", split_axis=0, concat_axis=0, tiled=True)
    halves = half_transform(blocks, col_counts, block_sizes, occ, FIRST, WIDTHS)
    weight = lax.dynamic_slice(occ_weight, (lax.axis_index("ten") * own,), (own,))
    used = jnp.sum(block_sizes)
    case = sum((used > tiles * LANES).astype(jnp.int32) for tiles in WIDTHS[:-1])
    return lax.switch(
        case,
        [functools.partial(finish, tiles) for tiles in WIDTHS],
        got, halves, block_sizes, weight, virt_green,
    )


def solution(mesh):
    return jax.shard_map(
        per_device,
        mesh=mesh,
        in_specs=(P(None, "ten", None), P(), P(), P(None, "rep"), P("rep"), P()),
        out_specs=P("ten", None),
        check_vma=False,
    )
```

```python
import functools

import jax
import jax.numpy as jnp
from jax import lax
from jax.experimental import pallas as pl
from jax.experimental.pallas import tpu as pltpu
from jax.sharding import PartitionSpec as P

BS = 64
MOST = 4
LANES = 128
MIB = 1024 * 1024
BUFFERS = 4
WIDTHS = (12, 13, 16)
FIRST = 4
LATER = 51


def prefix_sums(counts_ref, into):
    total = jnp.int32(0)
    for b in range(counts_ref.shape[0]):
        into[b] = total
        total = total + counts_ref[b]
    return total


def targets(position, sizes_ref, offsets, m):
    size0, size1 = sizes_ref[2 * m], sizes_ref[2 * m + 1]
    start = offsets[2 * m]
    second = position >= BS
    local = jnp.where(second, position - BS, position)
    place = (local + jnp.where(second, start + size0, start)) & (LANES - 1)
    return jnp.where(local < jnp.where(second, size1, size0), place, -1)


def half_kernel(lo, his, counts_ref, sizes_ref, occ_ref, blocks_ref, *refs):
    outs = refs[: len(his)]
    held, occ32, slots, turned, weights, carry, stage, starts, offsets, sems, out_sem = refs[len(his) :]
    block_count = counts_ref.shape[0]
    pair_count, aux_rows, _ = blocks_ref.shape
    occ_count = occ_ref.shape[1]
    half_x = BS // 2
    pitch = half_x + 1
    turned_pitch = aux_rows + 1
    window = 2 * MOST
    last_pair = block_count // 2

    prefix_sums(counts_ref, starts)
    used = prefix_sums(sizes_ref, offsets)
    hi = jnp.int32(his[-1])
    for smaller in reversed(his[:-1]):
        hi = jnp.where(used <= smaller * LANES, smaller, hi)

    def count_before(limit):
        return sum((offsets[2 * m] < limit).astype(jnp.int32) for m in range(last_pair))

    m_lo = jnp.int32(0) if lo == 0 else count_before(lo * LANES + 1) - 1
    m_hi = count_before(hi * LANES)

    def base_of(m):
        return jnp.minimum(starts[2 * m], pair_count - window)

    def fetch(m):
        slot = m & (BUFFERS - 1)
        return pltpu.make_async_copy(blocks_ref.at[pl.ds(base_of(m), window)], held.at[slot], sems.at[slot])

    for ahead in range(BUFFERS - 1):

        @pl.when(m_lo + ahead < m_hi)
        def _(ahead=ahead):
            fetch(m_lo + ahead).start()

    occ32[...] = occ_ref[...].astype(jnp.float32)
    slots[...] = jnp.zeros_like(slots)
    carry[...] = jnp.zeros_like(carry)
    turned[...] = jnp.zeros_like(turned)

    twice = 2 * lax.broadcasted_iota(jnp.int32, (half_x, occ_count), 0)
    low = lax.broadcasted_iota(jnp.int32, (BS, LANES), 1) < BS
    square_row = lax.broadcasted_iota(jnp.int32, (LANES, LANES), 0)
    square_lane = lax.broadcasted_iota(jnp.int32, (LANES, LANES), 1)

    def set_weights(m):
        for side in range(2):
            b = 2 * m + side
            count = counts_ref[b]
            rows = [[], []]
            for j in range(MOST):
                row = b + ((j + 1) // 2 if j % 2 == 1 else -(j // 2))
                row = jnp.where(row < 0, row + block_count, row)
                row = jnp.where(row >= block_count, row - block_count, row)
                size = jnp.where(j < count, sizes_ref[row], 0)
                for parity in range(2):
                    coeff = occ32[pl.ds(row * BS + parity, half_x, stride=2), :]
                    rows[parity].append(jnp.where(twice + parity < size, coeff, 0.0))
            for parity in range(2):
                weights[side, parity * occ_count : (parity + 1) * occ_count, :] = jnp.transpose(
                    jnp.concatenate(rows[parity], axis=0)
                ).astype(jnp.bfloat16)

    def turn_blocks(m):
        slot = m & (BUFFERS - 1)
        base = base_of(m)
        for side in range(2):
            first, count = starts[2 * m + side] - base, counts_ref[2 * m + side]
            for j in range(MOST):

                @pl.when(j < count)
                def _(side=side, j=j, first=first):
                    for t in range(half_x):
                        piece = held[slot, first + j, :, t * LANES : (t + 1) * LANES]
                        slots[side, j, pl.ds(t, aux_rows, stride=pitch), :] = piece.astype(jnp.float32)

    def multiply():
        for pp in range(aux_rows // 2):
            sums = []
            for side in range(2):
                cols = [
                    jnp.concatenate(
                        [slots[side, j, p * pitch : p * pitch + half_x, :] for j in range(MOST)], axis=0
                    ).astype(jnp.bfloat16)
                    for p in (2 * pp, 2 * pp + 1)
                ]
                sums.append(
                    jnp.dot(weights[side], jnp.concatenate(cols, axis=1), preferred_element_type=jnp.float32)
                )
            for q in range(2):
                even0 = sums[0][:BS, q * LANES : (q + 1) * LANES]
                odd0 = sums[0][BS:, q * LANES : (q + 1) * LANES]
                even1 = sums[1][:BS, q * LANES : (q + 1) * LANES]
                odd1 = sums[1][BS:, q * LANES : (q + 1) * LANES]
                turned[pl.ds(2 * pp + q, occ_count, stride=turned_pitch), :] = jnp.where(
                    low, even0, odd1
                ) + pltpu.roll(jnp.where(low, even1, odd0), BS, 1)

    def pack(m, valid):
        start = offsets[2 * m]
        tile, split = start >> 7, start & (LANES - 1)
        filled = split + sizes_ref[2 * m] + sizes_ref[2 * m + 1]
        full = valid & (filled >= LANES)
        select = square_lane == jnp.where(valid, targets(square_row, sizes_ref, offsets, m), -1)
        select = select.astype(jnp.bfloat16)
        here = square_lane >= split
        column = pl.ds(pl.multiple_of(jnp.maximum(tile - lo, 0) * LANES, LANES), LANES)
        group = LANES // aux_rows
        for g in range(occ_count // group):
            values = jnp.concatenate(
                [turned[i * turned_pitch : i * turned_pitch + aux_rows, :] for i in range(g * group, (g + 1) * group)],
                axis=0,
            ).astype(jnp.bfloat16)
            moved = jnp.dot(values, select, preferred_element_type=jnp.float32)
            rows = slice(g * LANES, (g + 1) * LANES)
            current = carry[rows, :] + jnp.where(here, moved, 0.0)
            stage[rows, column] = current.astype(jnp.bfloat16)
            carry[rows, :] = jnp.where(full, jnp.where(here, 0.0, moved), current)
        return jnp.where(filled > LANES, tile + 1, -1)

    set_weights(m_lo)

    def column_pair(m, state):
        @pl.when(m + BUFFERS - 1 < m_hi)
        def _():
            fetch(m + BUFFERS - 1).start()

        fetch(m).wait()
        turn_blocks(m)
        pack(jnp.maximum(m - 1, m_lo), m > m_lo)
        multiply()
        set_weights(jnp.minimum(m + 1, last_pair - 1))
        return state

    lax.fori_loop(m_lo, m_hi, column_pair, 0)
    spill = pack(m_hi - 1, m_hi > m_lo)

    def zero(tile, state):
        stage[:, pl.ds(pl.multiple_of((tile - lo) * LANES, LANES), LANES)] = jnp.zeros(
            (stage.shape[0], LANES), jnp.bfloat16
        )
        return state

    lax.fori_loop(jnp.maximum((used + LANES - 1) >> 7, lo), hi, zero, 0)

    @pl.when((spill >= lo) & (spill < hi))
    def _():
        stage[:, pl.ds(pl.multiple_of((spill - lo) * LANES, LANES), LANES)] = carry[...].astype(jnp.bfloat16)

    for out_ref, tiles in zip(outs, his):

        @pl.when(hi == tiles)
        def _(out_ref=out_ref, tiles=tiles):
            copy = pltpu.make_async_copy(stage.at[:, : (tiles - lo) * LANES], out_ref, out_sem)
            copy.start()
            copy.wait()


def half_transform(blocks, col_counts, block_sizes, occ, lo, his):
    pair_count, aux_rows, flat = blocks.shape
    block_count = col_counts.shape[0]
    occ_count = occ.shape[1]
    smem = pl.BlockSpec(memory_space=pltpu.SMEM)
    vmem = pl.BlockSpec(memory_space=pltpu.VMEM)
    hbm = pl.BlockSpec(memory_space=pltpu.HBM)
    return pl.pallas_call(
        functools.partial(half_kernel, lo, his),
        out_shape=[jax.ShapeDtypeStruct((occ_count * aux_rows, (hi - lo) * LANES), jnp.bfloat16) for hi in his],
        in_specs=[smem, smem, vmem, hbm],
        out_specs=[hbm] * len(his),
        scratch_shapes=[
            pltpu.VMEM((BUFFERS, 2 * MOST, aux_rows, flat), jnp.bfloat16),
            pltpu.VMEM(occ.shape, jnp.float32),
            pltpu.VMEM((2, MOST, aux_rows * (BS // 2 + 1), LANES), jnp.float32),
            pltpu.VMEM((occ_count * (aux_rows + 1), LANES), jnp.float32),
            pltpu.VMEM((2, 2 * occ_count, MOST * BS // 2), jnp.bfloat16),
            pltpu.VMEM((occ_count * aux_rows, LANES), jnp.float32),
            pltpu.VMEM((occ_count * aux_rows, (his[-1] - lo) * LANES), jnp.bfloat16),
            pltpu.SMEM((block_count,), jnp.int32),
            pltpu.SMEM((block_count,), jnp.int32),
            pltpu.SemaphoreType.DMA((BUFFERS,)),
            pltpu.SemaphoreType.DMA,
        ],
        compiler_params=pltpu.CompilerParams(vmem_limit_bytes=60 * MIB),
        cost_estimate=pl.CostEstimate(flops=8 * 10**9, bytes_accessed=8 * MIB, transcendentals=0),
        name="half_transform",
    )(col_counts, block_sizes, occ, blocks)


def pack_kernel(sizes_ref, green_ref, out_ref, packed_rows, row_carry, lane_carry, offsets):
    basis_count = green_ref.shape[0]
    width = out_ref.shape[0]
    last_pair = sizes_ref.shape[0] // 2
    used = prefix_sums(sizes_ref, offsets)
    tiles = (used + LANES - 1) >> 7
    square_row = lax.broadcasted_iota(jnp.int32, (LANES, LANES), 0)
    square_lane = lax.broadcasted_iota(jnp.int32, (LANES, LANES), 1)
    strip = 4 * LANES
    row_carry[...] = jnp.zeros_like(row_carry)
    lane_carry[...] = jnp.zeros_like(lane_carry)

    def place(m):
        start = offsets[2 * m]
        split = start & (LANES - 1)
        return start >> 7, split, split + sizes_ref[2 * m] + sizes_ref[2 * m + 1]

    def at(tile):
        return pl.ds(pl.multiple_of(tile * LANES, LANES), LANES)

    def pack_rows(m, state):
        tile, split, filled = place(m)
        select = (square_row == targets(square_lane, sizes_ref, offsets, m)).astype(jnp.bfloat16)
        here = lax.broadcasted_iota(jnp.int32, (LANES, strip), 0) >= split
        for s in range(basis_count // strip):
            lanes = slice(s * strip, (s + 1) * strip)
            moved = jnp.dot(select, green_ref[at(m), lanes], preferred_element_type=jnp.float32)
            current = row_carry[:, lanes] + jnp.where(here, moved, 0.0)
            packed_rows[at(tile), lanes] = current.astype(jnp.bfloat16)
            row_carry[:, lanes] = jnp.where(filled >= LANES, jnp.where(here, 0.0, moved), current)
        return jnp.where(filled > LANES, tile + 1, -1)

    spill = lax.fori_loop(0, last_pair, pack_rows, jnp.int32(-1))

    def zero_rows(tile, state):
        packed_rows[at(tile), :] = jnp.zeros((LANES, basis_count), jnp.bfloat16)
        return state

    lax.fori_loop(tiles, width // LANES, zero_rows, 0)

    @pl.when(spill >= 0)
    def _():
        packed_rows[at(spill), :] = row_carry[...].astype(jnp.bfloat16)

    def pack_lanes(m, state):
        tile, split, filled = place(m)
        select = (square_lane == targets(square_row, sizes_ref, offsets, m)).astype(jnp.bfloat16)
        here = square_lane >= split
        for r in range(width // LANES):
            rows = slice(r * LANES, (r + 1) * LANES)
            moved = jnp.dot(packed_rows[rows, at(m)], select, preferred_element_type=jnp.float32)
            current = lane_carry[rows, :] + jnp.where(here, moved, 0.0)
            out_ref[rows, at(tile)] = current.astype(jnp.bfloat16)
            lane_carry[rows, :] = jnp.where(filled >= LANES, jnp.where(here, 0.0, moved), current)
        return state

    lax.fori_loop(0, last_pair, pack_lanes, 0)

    def zero_lanes(tile, state):
        out_ref[:, at(tile)] = jnp.zeros((width, LANES), jnp.bfloat16)
        return state

    lax.fori_loop(tiles, width // LANES, zero_lanes, 0)

    @pl.when(spill >= 0)
    def _():
        out_ref[:, at(spill)] = lane_carry[...].astype(jnp.bfloat16)


def pack_green(block_sizes, virt_green, width):
    basis_count = virt_green.shape[0]
    vmem = pl.BlockSpec(memory_space=pltpu.VMEM)
    return pl.pallas_call(
        pack_kernel,
        out_shape=jax.ShapeDtypeStruct((width, width), jnp.bfloat16),
        in_specs=[pl.BlockSpec(memory_space=pltpu.SMEM), vmem],
        out_specs=vmem,
        scratch_shapes=[
            pltpu.VMEM((width, basis_count), jnp.bfloat16),
            pltpu.VMEM((LANES, basis_count), jnp.float32),
            pltpu.VMEM((width, LANES), jnp.float32),
            pltpu.SMEM((block_sizes.shape[0],), jnp.int32),
        ],
        compiler_params=pltpu.CompilerParams(vmem_limit_bytes=60 * MIB),
        cost_estimate=pl.CostEstimate(flops=10 * 10**9, bytes_accessed=14 * MIB, transcendentals=0),
        name="pack_green",
    )(block_sizes, virt_green)


def dress_kernel(half_ref, green_ref, out_ref):
    sources, own, aux_rows, depth = half_ref.shape
    rows = sources * aux_rows
    for ii in range(own):
        out_ref[ii] = jnp.dot(
            half_ref[:, ii].reshape(rows, depth), green_ref[...], preferred_element_type=jnp.float32
        )


def column_start(step, tile, width):
    return pl.multiple_of(jnp.minimum(step * tile, width - tile), LANES)


def dress(half, green, tile):
    sources, own, aux_rows, depth = half.shape
    rows = sources * aux_rows
    width = green.shape[1]
    steps = pl.cdiv(width, tile)
    return pl.pallas_call(
        dress_kernel,
        grid=(steps,),
        out_shape=jax.ShapeDtypeStruct((own, rows, steps * tile), jnp.float32),
        in_specs=[
            pl.BlockSpec((sources, own, aux_rows, depth), lambda n: (0, 0, 0, 0)),
            pl.BlockSpec((pl.Element(depth), pl.Element(tile)), lambda n: (0, column_start(n, tile, width))),
        ],
        out_specs=pl.BlockSpec((own, rows, tile), lambda n: (0, 0, n)),
        compiler_params=pltpu.CompilerParams(vmem_limit_bytes=60 * MIB),
        cost_estimate=pl.CostEstimate(
            flops=2 * own * rows * depth * width,
            bytes_accessed=2 * own * rows * depth + 2 * depth * width + 4 * own * rows * width,
            transcendentals=0,
        ),
        name="dress",
    )(half, green)


def response_kernel(split, width, weight_ref, half0_ref, half1_ref, green_ref, part_ref, chi_ref, total):
    step = pl.program_id(0)
    sources, own, aux_rows, depth = half1_ref.shape
    rows = sources * aux_rows
    tile = green_ref.shape[1]
    start = column_start(step, tile, width)
    fresh = lax.broadcasted_iota(jnp.int32, (rows, tile), 1) >= step * tile - start

    @pl.when(step == 0)
    def _():
        total[...] = jnp.zeros_like(total)

    def add(half_ref, first):
        columns = pl.ds(pl.multiple_of(start - first, LANES), tile)
        left, right = [], []
        for ii in range(own):
            dressed = part_ref[ii] + jnp.dot(
                half1_ref[:, ii].reshape(rows, depth), green_ref[...], preferred_element_type=jnp.float32
            )
            right.append(jnp.where(fresh, dressed * weight_ref[ii], 0.0).astype(jnp.bfloat16))
            left.append(half_ref[:, ii, :, columns].reshape(rows, tile))
        total[...] += lax.dot_general(
            jnp.concatenate(left, axis=1),
            jnp.concatenate(right, axis=1),
            (((1,), (1,)), ((), ())),
            preferred_element_type=jnp.float32,
        )

    @pl.when(step < split // tile)
    def _():
        add(half0_ref, 0)

    @pl.when(step >= split // tile)
    def _():
        add(half1_ref, split)

    @pl.when(step == pl.num_programs(0) - 1)
    def _():
        chi_ref[...] = total[...].astype(chi_ref.dtype)


def response(half0, half1, weight, part, green, tile):
    sources, own, aux_rows, depth0 = half0.shape
    depth1 = half1.shape[3]
    rows = sources * aux_rows
    width = depth0 + depth1
    whole = lambda n: (0, 0, 0, 0)
    return pl.pallas_call(
        functools.partial(response_kernel, depth0, width),
        grid=(pl.cdiv(width, tile),),
        out_shape=jax.ShapeDtypeStruct((rows, rows), jnp.bfloat16),
        in_specs=[
            pl.BlockSpec(memory_space=pltpu.SMEM),
            pl.BlockSpec((sources, own, aux_rows, depth0), whole),
            pl.BlockSpec((sources, own, aux_rows, depth1), whole),
            pl.BlockSpec((pl.Element(depth1), pl.Element(tile)), lambda n: (depth0, column_start(n, tile, width))),
            pl.BlockSpec((own, rows, tile), lambda n: (0, 0, n)),
        ],
        out_specs=pl.BlockSpec((rows, rows), lambda n: (0, 0)),
        scratch_shapes=[pltpu.VMEM((rows, rows), jnp.float32)],
        compiler_params=pltpu.CompilerParams(vmem_limit_bytes=LATER * MIB),
        name="response",
    )(weight, half0, half1, green, part)


def finish(tiles, got, halves, block_sizes, weight, virt_green):
    devices, own, aux_rows, _ = got.shape
    half = halves[WIDTHS.index(tiles)].reshape(devices, own, aux_rows, (tiles - FIRST) * LANES)
    rest = lax.all_to_all(half, "ten", split_axis=0, concat_axis=0, tiled=True)
    green = pack_green(block_sizes, virt_green, tiles * LANES)
    tile = 512 if tiles % 4 == 0 else 256
    part = dress(got, green, tile)
    terms = response(got, rest, weight, part, green, tile).reshape(devices, aux_rows, devices * aux_rows)
    terms = lax.all_to_all(terms, "ten", split_axis=0, concat_axis=0, tiled=True)
    share = jnp.sum(terms.astype(jnp.float32), axis=0)
    groups = lax.axis_size("rep")
    one, two, three = (
        lax.ppermute(share, "rep", [(z, (z + step) % groups) for z in range(groups)]) for step in (1, 2, 3)
    )
    return (share + two) + (one + three)


def per_device(blocks, col_counts, block_sizes, occ_coeff, occ_weight, virt_green):
    devices = lax.axis_size("ten")
    aux_rows = blocks.shape[1]
    own = occ_coeff.shape[1] // devices
    (half,) = half_transform(blocks, col_counts, block_sizes, occ_coeff, 0, (FIRST,))
    half = half.reshape(devices, own, aux_rows, FIRST * LANES)
    got = lax.all_to_all(half, "ten", split_axis=0, concat_axis=0, tiled=True)
    halves = half_transform(blocks, col_counts, block_sizes, occ_coeff, FIRST, WIDTHS)
    weight = lax.dynamic_slice(occ_weight, (lax.axis_index("ten") * own,), (own,))
    used = jnp.sum(block_sizes)
    case = sum((used > tiles * LANES).astype(jnp.int32) for tiles in WIDTHS[:-1])
    return lax.switch(
        case,
        [functools.partial(finish, tiles) for tiles in WIDTHS],
        got, halves, block_sizes, weight, virt_green,
    )


def solution(mesh):
    return jax.shard_map(
        per_device,
        mesh=mesh,
        in_specs=(P(None, "ten", None), P(), P(), P(None, "rep"), P("rep"), P()),
        out_specs=P("ten", None),
        check_vma=False,
    )
```

```python
import functools

import jax
import jax.numpy as jnp
from jax import lax
from jax.experimental import pallas as pl
from jax.experimental.pallas import tpu as pltpu
from jax.sharding import PartitionSpec as P

BS = 64
MOST = 4
LANES = 128
MIB = 1024 * 1024
BUFFERS = 4
WIDTHS = (12, 13, 16)
FIRST = 4
LATER = 51


def prefix_sums(counts_ref, into):
    total = jnp.int32(0)
    for b in range(counts_ref.shape[0]):
        into[b] = total
        total = total + counts_ref[b]
    return total


def targets(position, sizes_ref, offsets, m):
    size0, size1 = sizes_ref[2 * m], sizes_ref[2 * m + 1]
    start = offsets[2 * m]
    second = position >= BS
    local = jnp.where(second, position - BS, position)
    place = (local + jnp.where(second, start + size0, start)) & (LANES - 1)
    return jnp.where(local < jnp.where(second, size1, size0), place, -1)


def half_kernel(lo, his, counts_ref, sizes_ref, occ_ref, blocks_ref, *refs):
    outs = refs[: len(his)]
    held, occ32, slots, turned, weights, carry, stage, starts, offsets, sems, out_sem = refs[len(his) :]
    block_count = counts_ref.shape[0]
    pair_count, aux_rows, _ = blocks_ref.shape
    occ_count = occ_ref.shape[0]
    half_x = BS // 2
    pitch = half_x + 1
    turned_pitch = aux_rows + 1
    window = 2 * MOST
    last_pair = block_count // 2

    prefix_sums(counts_ref, starts)
    used = prefix_sums(sizes_ref, offsets)
    hi = jnp.int32(his[-1])
    for smaller in reversed(his[:-1]):
        hi = jnp.where(used <= smaller * LANES, smaller, hi)

    def count_before(limit):
        return sum((offsets[2 * m] < limit).astype(jnp.int32) for m in range(last_pair))

    m_lo = jnp.int32(0) if lo == 0 else count_before(lo * LANES + 1) - 1
    m_hi = count_before(hi * LANES)

    def base_of(m):
        return jnp.minimum(starts[2 * m], pair_count - window)

    def fetch(m):
        slot = m & (BUFFERS - 1)
        return pltpu.make_async_copy(blocks_ref.at[pl.ds(base_of(m), window)], held.at[slot], sems.at[slot])

    for ahead in range(BUFFERS - 1):

        @pl.when(m_lo + ahead < m_hi)
        def _(ahead=ahead):
            fetch(m_lo + ahead).start()

    for c in range(occ_ref.shape[1] // LANES):
        columns = slice(c * LANES, (c + 1) * LANES)
        occ32[columns, :] = jnp.transpose(occ_ref[:, columns].astype(jnp.float32))
    slots[...] = jnp.zeros_like(slots)
    carry[...] = jnp.zeros_like(carry)
    turned[...] = jnp.zeros_like(turned)

    twice = 2 * lax.broadcasted_iota(jnp.int32, (half_x, occ_count), 0)
    low = lax.broadcasted_iota(jnp.int32, (BS, LANES), 1) < BS
    square_row = lax.broadcasted_iota(jnp.int32, (LANES, LANES), 0)
    square_lane = lax.broadcasted_iota(jnp.int32, (LANES, LANES), 1)

    def set_weights(m):
        for side in range(2):
            b = 2 * m + side
            count = counts_ref[b]
            rows = [[], []]
            for j in range(MOST):
                row = b + ((j + 1) // 2 if j % 2 == 1 else -(j // 2))
                row = jnp.where(row < 0, row + block_count, row)
                row = jnp.where(row >= block_count, row - block_count, row)
                size = jnp.where(j < count, sizes_ref[row], 0)
                for parity in range(2):
                    coeff = occ32[pl.ds(row * BS + parity, half_x, stride=2), :]
                    rows[parity].append(jnp.where(twice + parity < size, coeff, 0.0))
            for parity in range(2):
                weights[side, parity * occ_count : (parity + 1) * occ_count, :] = jnp.transpose(
                    jnp.concatenate(rows[parity], axis=0)
                ).astype(jnp.bfloat16)

    def turn_blocks(m):
        slot = m & (BUFFERS - 1)
        base = base_of(m)
        for side in range(2):
            first, count = starts[2 * m + side] - base, counts_ref[2 * m + side]
            for j in range(MOST):

                @pl.when(j < count)
                def _(side=side, j=j, first=first):
                    for t in range(half_x):
                        piece = held[slot, first + j, :, t * LANES : (t + 1) * LANES]
                        slots[side, j, pl.ds(t, aux_rows, stride=pitch), :] = piece.astype(jnp.float32)

    def multiply():
        for pp in range(aux_rows // 2):
            sums = []
            for side in range(2):
                cols = [
                    jnp.concatenate(
                        [slots[side, j, p * pitch : p * pitch + half_x, :] for j in range(MOST)], axis=0
                    ).astype(jnp.bfloat16)
                    for p in (2 * pp, 2 * pp + 1)
                ]
                sums.append(
                    jnp.dot(weights[side], jnp.concatenate(cols, axis=1), preferred_element_type=jnp.float32)
                )
            for q in range(2):
                even0 = sums[0][:BS, q * LANES : (q + 1) * LANES]
                odd0 = sums[0][BS:, q * LANES : (q + 1) * LANES]
                even1 = sums[1][:BS, q * LANES : (q + 1) * LANES]
                odd1 = sums[1][BS:, q * LANES : (q + 1) * LANES]
                turned[pl.ds(2 * pp + q, occ_count, stride=turned_pitch), :] = jnp.where(
                    low, even0, odd1
                ) + pltpu.roll(jnp.where(low, even1, odd0), BS, 1)

    def pack(m, valid):
        start = offsets[2 * m]
        tile, split = start >> 7, start & (LANES - 1)
        filled = split + sizes_ref[2 * m] + sizes_ref[2 * m + 1]
        full = valid & (filled >= LANES)
        select = square_lane == jnp.where(valid, targets(square_row, sizes_ref, offsets, m), -1)
        select = select.astype(jnp.bfloat16)
        here = square_lane >= split
        column = pl.ds(pl.multiple_of(jnp.maximum(tile - lo, 0) * LANES, LANES), LANES)
        group = LANES // aux_rows
        for g in range(occ_count // group):
            values = jnp.concatenate(
                [turned[i * turned_pitch : i * turned_pitch + aux_rows, :] for i in range(g * group, (g + 1) * group)],
                axis=0,
            ).astype(jnp.bfloat16)
            moved = jnp.dot(values, select, preferred_element_type=jnp.float32)
            rows = slice(g * LANES, (g + 1) * LANES)
            current = carry[rows, :] + jnp.where(here, moved, 0.0)
            stage[rows, column] = current.astype(jnp.bfloat16)
            carry[rows, :] = jnp.where(full, jnp.where(here, 0.0, moved), current)
        return jnp.where(filled > LANES, tile + 1, -1)

    set_weights(m_lo)

    def column_pair(m, state):
        @pl.when(m + BUFFERS - 1 < m_hi)
        def _():
            fetch(m + BUFFERS - 1).start()

        fetch(m).wait()
        turn_blocks(m)
        pack(jnp.maximum(m - 1, m_lo), m > m_lo)
        multiply()
        set_weights(jnp.minimum(m + 1, last_pair - 1))
        return state

    lax.fori_loop(m_lo, m_hi, column_pair, 0)
    spill = pack(m_hi - 1, m_hi > m_lo)

    def zero(tile, state):
        stage[:, pl.ds(pl.multiple_of((tile - lo) * LANES, LANES), LANES)] = jnp.zeros(
            (stage.shape[0], LANES), jnp.bfloat16
        )
        return state

    lax.fori_loop(jnp.maximum((used + LANES - 1) >> 7, lo), hi, zero, 0)

    @pl.when((spill >= lo) & (spill < hi))
    def _():
        stage[:, pl.ds(pl.multiple_of((spill - lo) * LANES, LANES), LANES)] = carry[...].astype(jnp.bfloat16)

    for out_ref, tiles in zip(outs, his):

        @pl.when(hi == tiles)
        def _(out_ref=out_ref, tiles=tiles):
            copy = pltpu.make_async_copy(stage.at[:, : (tiles - lo) * LANES], out_ref, out_sem)
            copy.start()
            copy.wait()


def half_transform(blocks, col_counts, block_sizes, occ, lo, his):
    pair_count, aux_rows, flat = blocks.shape
    block_count = col_counts.shape[0]
    occ_count = occ.shape[1]
    smem = pl.BlockSpec(memory_space=pltpu.SMEM)
    vmem = pl.BlockSpec(memory_space=pltpu.VMEM)
    hbm = pl.BlockSpec(memory_space=pltpu.HBM)
    return pl.pallas_call(
        functools.partial(half_kernel, lo, his),
        out_shape=[jax.ShapeDtypeStruct((occ_count * aux_rows, (hi - lo) * LANES), jnp.bfloat16) for hi in his],
        in_specs=[smem, smem, vmem, hbm],
        out_specs=[hbm] * len(his),
        scratch_shapes=[
            pltpu.VMEM((BUFFERS, 2 * MOST, aux_rows, flat), jnp.bfloat16),
            pltpu.VMEM(occ.shape, jnp.float32),
            pltpu.VMEM((2, MOST, aux_rows * (BS // 2 + 1), LANES), jnp.float32),
            pltpu.VMEM((occ_count * (aux_rows + 1), LANES), jnp.float32),
            pltpu.VMEM((2, 2 * occ_count, MOST * BS // 2), jnp.bfloat16),
            pltpu.VMEM((occ_count * aux_rows, LANES), jnp.float32),
            pltpu.VMEM((occ_count * aux_rows, (his[-1] - lo) * LANES), jnp.bfloat16),
            pltpu.SMEM((block_count,), jnp.int32),
            pltpu.SMEM((block_count,), jnp.int32),
            pltpu.SemaphoreType.DMA((BUFFERS,)),
            pltpu.SemaphoreType.DMA,
        ],
        compiler_params=pltpu.CompilerParams(vmem_limit_bytes=60 * MIB),
        cost_estimate=pl.CostEstimate(flops=8 * 10**9, bytes_accessed=8 * MIB, transcendentals=0),
        name="half_transform",
    )(col_counts, block_sizes, occ.T, blocks)


def pack_kernel(sizes_ref, green_ref, out_ref, packed_rows, row_carry, lane_carry, offsets):
    basis_count = green_ref.shape[0]
    width = out_ref.shape[0]
    last_pair = sizes_ref.shape[0] // 2
    used = prefix_sums(sizes_ref, offsets)
    tiles = (used + LANES - 1) >> 7
    square_row = lax.broadcasted_iota(jnp.int32, (LANES, LANES), 0)
    square_lane = lax.broadcasted_iota(jnp.int32, (LANES, LANES), 1)
    strip = 4 * LANES
    row_carry[...] = jnp.zeros_like(row_carry)
    lane_carry[...] = jnp.zeros_like(lane_carry)

    def place(m):
        start = offsets[2 * m]
        split = start & (LANES - 1)
        return start >> 7, split, split + sizes_ref[2 * m] + sizes_ref[2 * m + 1]

    def at(tile):
        return pl.ds(pl.multiple_of(tile * LANES, LANES), LANES)

    def pack_rows(m, state):
        tile, split, filled = place(m)
        select = (square_row == targets(square_lane, sizes_ref, offsets, m)).astype(jnp.bfloat16)
        here = lax.broadcasted_iota(jnp.int32, (LANES, strip), 0) >= split
        for s in range(basis_count // strip):
            lanes = slice(s * strip, (s + 1) * strip)
            moved = jnp.dot(select, green_ref[at(m), lanes], preferred_element_type=jnp.float32)
            current = row_carry[:, lanes] + jnp.where(here, moved, 0.0)
            packed_rows[at(tile), lanes] = current.astype(jnp.bfloat16)
            row_carry[:, lanes] = jnp.where(filled >= LANES, jnp.where(here, 0.0, moved), current)
        return jnp.where(filled > LANES, tile + 1, -1)

    spill = lax.fori_loop(0, last_pair, pack_rows, jnp.int32(-1))

    def zero_rows(tile, state):
        packed_rows[at(tile), :] = jnp.zeros((LANES, basis_count), jnp.bfloat16)
        return state

    lax.fori_loop(tiles, width // LANES, zero_rows, 0)

    @pl.when(spill >= 0)
    def _():
        packed_rows[at(spill), :] = row_carry[...].astype(jnp.bfloat16)

    def pack_lanes(m, state):
        tile, split, filled = place(m)
        select = (square_lane == targets(square_row, sizes_ref, offsets, m)).astype(jnp.bfloat16)
        here = square_lane >= split
        for r in range(width // LANES):
            rows = slice(r * LANES, (r + 1) * LANES)
            moved = jnp.dot(packed_rows[rows, at(m)], select, preferred_element_type=jnp.float32)
            current = lane_carry[rows, :] + jnp.where(here, moved, 0.0)
            out_ref[rows, at(tile)] = current.astype(jnp.bfloat16)
            lane_carry[rows, :] = jnp.where(filled >= LANES, jnp.where(here, 0.0, moved), current)
        return state

    lax.fori_loop(0, last_pair, pack_lanes, 0)

    def zero_lanes(tile, state):
        out_ref[:, at(tile)] = jnp.zeros((width, LANES), jnp.bfloat16)
        return state

    lax.fori_loop(tiles, width // LANES, zero_lanes, 0)

    @pl.when(spill >= 0)
    def _():
        out_ref[:, at(spill)] = lane_carry[...].astype(jnp.bfloat16)


def pack_green(block_sizes, virt_green, width):
    basis_count = virt_green.shape[0]
    vmem = pl.BlockSpec(memory_space=pltpu.VMEM)
    return pl.pallas_call(
        pack_kernel,
        out_shape=jax.ShapeDtypeStruct((width, width), jnp.bfloat16),
        in_specs=[pl.BlockSpec(memory_space=pltpu.SMEM), vmem],
        out_specs=vmem,
        scratch_shapes=[
            pltpu.VMEM((width, basis_count), jnp.bfloat16),
            pltpu.VMEM((LANES, basis_count), jnp.float32),
            pltpu.VMEM((width, LANES), jnp.float32),
            pltpu.SMEM((block_sizes.shape[0],), jnp.int32),
        ],
        compiler_params=pltpu.CompilerParams(vmem_limit_bytes=60 * MIB),
        cost_estimate=pl.CostEstimate(flops=10 * 10**9, bytes_accessed=14 * MIB, transcendentals=0),
        name="pack_green",
    )(block_sizes, virt_green)


def dress_kernel(half_ref, green_ref, out_ref):
    sources, own, aux_rows, depth = half_ref.shape
    rows = sources * aux_rows
    for ii in range(own):
        out_ref[ii] = jnp.dot(
            half_ref[:, ii].reshape(rows, depth), green_ref[...], preferred_element_type=jnp.float32
        )


def column_start(step, tile, width):
    return pl.multiple_of(jnp.minimum(step * tile, width - tile), LANES)


def dress(half, green, tile):
    sources, own, aux_rows, depth = half.shape
    rows = sources * aux_rows
    width = green.shape[1]
    steps = pl.cdiv(width, tile)
    return pl.pallas_call(
        dress_kernel,
        grid=(steps,),
        out_shape=jax.ShapeDtypeStruct((own, rows, steps * tile), jnp.float32),
        in_specs=[
            pl.BlockSpec((sources, own, aux_rows, depth), lambda n: (0, 0, 0, 0)),
            pl.BlockSpec((pl.Element(depth), pl.Element(tile)), lambda n: (0, column_start(n, tile, width))),
        ],
        out_specs=pl.BlockSpec((own, rows, tile), lambda n: (0, 0, n)),
        compiler_params=pltpu.CompilerParams(vmem_limit_bytes=60 * MIB),
        cost_estimate=pl.CostEstimate(
            flops=2 * own * rows * depth * width,
            bytes_accessed=2 * own * rows * depth + 2 * depth * width + 4 * own * rows * width,
            transcendentals=0,
        ),
        name="dress",
    )(half, green)


def response_kernel(split, width, weight_ref, half0_ref, half1_ref, green_ref, part_ref, chi_ref, total):
    step = pl.program_id(0)
    sources, own, aux_rows, depth = half1_ref.shape
    rows = sources * aux_rows
    tile = green_ref.shape[1]
    start = column_start(step, tile, width)
    fresh = lax.broadcasted_iota(jnp.int32, (rows, tile), 1) >= step * tile - start

    @pl.when(step == 0)
    def _():
        total[...] = jnp.zeros_like(total)

    def add(half_ref, first):
        columns = pl.ds(pl.multiple_of(start - first, LANES), tile)
        left, right = [], []
        for ii in range(own):
            dressed = part_ref[ii] + jnp.dot(
                half1_ref[:, ii].reshape(rows, depth), green_ref[...], preferred_element_type=jnp.float32
            )
            right.append(jnp.where(fresh, dressed * weight_ref[ii], 0.0).astype(jnp.bfloat16))
            left.append(half_ref[:, ii, :, columns].reshape(rows, tile))
        total[...] += lax.dot_general(
            jnp.concatenate(left, axis=1),
            jnp.concatenate(right, axis=1),
            (((1,), (1,)), ((), ())),
            preferred_element_type=jnp.float32,
        )

    @pl.when(step < split // tile)
    def _():
        add(half0_ref, 0)

    @pl.when(step >= split // tile)
    def _():
        add(half1_ref, split)

    @pl.when(step == pl.num_programs(0) - 1)
    def _():
        chi_ref[...] = total[...].astype(chi_ref.dtype)


def response(half0, half1, weight, part, green, tile):
    sources, own, aux_rows, depth0 = half0.shape
    depth1 = half1.shape[3]
    rows = sources * aux_rows
    width = depth0 + depth1
    whole = lambda n: (0, 0, 0, 0)
    return pl.pallas_call(
        functools.partial(response_kernel, depth0, width),
        grid=(pl.cdiv(width, tile),),
        out_shape=jax.ShapeDtypeStruct((rows, rows), jnp.bfloat16),
        in_specs=[
            pl.BlockSpec(memory_space=pltpu.SMEM),
            pl.BlockSpec((sources, own, aux_rows, depth0), whole),
            pl.BlockSpec((sources, own, aux_rows, depth1), whole),
            pl.BlockSpec((pl.Element(depth1), pl.Element(tile)), lambda n: (depth0, column_start(n, tile, width))),
            pl.BlockSpec((own, rows, tile), lambda n: (0, 0, n)),
        ],
        out_specs=pl.BlockSpec((rows, rows), lambda n: (0, 0)),
        scratch_shapes=[pltpu.VMEM((rows, rows), jnp.float32)],
        compiler_params=pltpu.CompilerParams(vmem_limit_bytes=LATER * MIB),
        name="response",
    )(weight, half0, half1, green, part)


def finish(tiles, got, halves, block_sizes, weight, virt_green):
    devices, own, aux_rows, _ = got.shape
    half = halves[WIDTHS.index(tiles)].reshape(devices, own, aux_rows, (tiles - FIRST) * LANES)
    rest = lax.all_to_all(half, "ten", split_axis=0, concat_axis=0, tiled=True)
    green = pack_green(block_sizes, virt_green, tiles * LANES)
    tile = 512 if tiles % 4 == 0 else 256
    part = dress(got, green, tile)
    terms = response(got, rest, weight, part, green, tile).reshape(devices, aux_rows, devices * aux_rows)
    terms = lax.all_to_all(terms, "ten", split_axis=0, concat_axis=0, tiled=True)
    share = jnp.sum(terms.astype(jnp.float32), axis=0)
    groups = lax.axis_size("rep")
    one, two, three = (
        lax.ppermute(share, "rep", [(z, (z + step) % groups) for z in range(groups)]) for step in (1, 2, 3)
    )
    return (share + two) + (one + three)


def per_device(blocks, col_counts, block_sizes, occ_coeff, occ_weight, virt_green):
    devices = lax.axis_size("ten")
    aux_rows = blocks.shape[1]
    own = occ_coeff.shape[1] // devices
    (half,) = half_transform(blocks, col_counts, block_sizes, occ_coeff, 0, (FIRST,))
    half = half.reshape(devices, own, aux_rows, FIRST * LANES)
    got = lax.all_to_all(half, "ten", split_axis=0, concat_axis=0, tiled=True)
    halves = half_transform(blocks, col_counts, block_sizes, occ_coeff, FIRST, WIDTHS)
    weight = lax.dynamic_slice(occ_weight, (lax.axis_index("ten") * own,), (own,))
    used = jnp.sum(block_sizes)
    case = sum((used > tiles * LANES).astype(jnp.int32) for tiles in WIDTHS[:-1])
    return lax.switch(
        case,
        [functools.partial(finish, tiles) for tiles in WIDTHS],
        got, halves, block_sizes, weight, virt_green,
    )


def solution(mesh):
    return jax.shard_map(
        per_device,
        mesh=mesh,
        in_specs=(P(None, "ten", None), P(), P(), P(None, "rep"), P("rep"), P()),
        out_specs=P("ten", None),
        check_vma=False,
    )
```
